256 devices in a mesh: grid: 64 (over z, y_hi, x), head: 4 (over y_lo, core).
Axes of the slice: x: 4, y: 4 (y_hi: 2, y_lo: 2; y = y_hi * 2 + y_lo), z: 8, core: 2. Of those that a mesh axis runs over, the one named last changes fastest.
Arguments:
- hidden_in: bfloat16 [64, 32, 16, 1024], P('grid', 'head'), may hold values from -16 to 16
- queries: bfloat16 [64, 32, 16, 1024], P('grid', None, None, 'head'), may hold values from -8 to 8
- keys: bfloat16 [64, 32, 16, 1024], P('grid', None, None, 'head'), may hold values from -8 to 8
- values: bfloat16 [64, 32, 16, 1024], P('grid', None, None, 'head'), may hold values from -6 to 6
- w_qkv: bfloat16 [1024, 3, 1024], P(None, None, 'head'), may hold values from -0.1875 to 0.1875
- w_out: bfloat16 [1024, 1024], P('head'), may hold values from -0.1875 to 0.1875
- out_grad: bfloat16 [64, 32, 16, 1024], P('grid', 'head'), may hold values from -16 to 16
Outputs:
- grad_hidden: bfloat16 [64, 32, 16, 1024], P('grid', 'head')
- grad_wqkv: float32 [1024, 3, 1024], P('grid', None, 'head')
- grad_wout: float32 [1024, 1024], P('head', 'grid')
The draws below stay inside these ranges and needn't reach their ends.
All inputs are finite; a program needn't handle non-finite values.
Results may differ from the reference program's by a relative error of at most 0.027.
Values may be sent and summed in bfloat16 or wider, within the bound.
No kernel may reach another device: no remote copies, remote signals or barrier semaphores. Data moves between devices by JAX's collectives and lax.ppermute only.
A program may use at most 128 MiB of HBM per device.

```python
import jax
import jax.numpy as jnp
from jax import lax

D = 1024
HEADS = 16
HD = 64
WIN = 7
TILE_COLS = 8
TH = 32
TW = 16
TILES = 64
TILE_ROWS = 8
IMG_H = 256
IMG_W = 128


def draw_queries(key, part):
    key = jax.random.fold_in(key, 1)
    base = jnp.clip(jax.random.normal(key, (TILES, TH, TW, D), jnp.float32), -8.0, 8.0)
    return base.astype(jnp.bfloat16)


def draw_keys(key, part):
    key = jax.random.fold_in(key, 2)
    base = jnp.clip(jax.random.normal(key, (TILES, TH, TW, D), jnp.float32), -8.0, 8.0)
    return base.astype(jnp.bfloat16)


def with_spikes(drawn, own_key, source, target, parts, factor):
    owner, partner = [(jnp.arange(drawn.shape[axis_at]) // (drawn.shape[axis_at] // parts)).reshape([-1 if axis == axis_at else 1 for axis in range(drawn.ndim)]) for axis_at in (source, target)]
    chosen = jax.random.permutation(own_key, parts)[partner]
    strong = (owner == chosen) | (owner == (partner + parts // 2) % parts)
    return jnp.where(strong, factor * drawn, drawn)


def levels(stream_key, shape, pieces, low, top_value):
    def one(dim, blocks):
        draws = jax.random.uniform(jax.random.fold_in(jax.random.fold_in(stream_key, 6), dim), (blocks,), jnp.float32, low / len(pieces), top_value / len(pieces))
        return jnp.repeat(jnp.exp(draws), shape[dim] // blocks).reshape((-1,) + (1,) * (len(shape) - dim - 1))

    loudness = one(*pieces[0])
    for cut in pieces[1:]:
        loudness = loudness * one(*cut)
    return loudness


def gaussian(stream_key, extent, width, bound, cuts=(), held_as=jnp.bfloat16):
    drawn = width * jax.random.normal(stream_key, extent, jnp.float32)
    if cuts:
        drawn = drawn * levels(stream_key, extent, cuts, -0.22, 0.18)
    return jnp.clip(drawn, -bound, bound).astype(held_as)


def gaussian_with(stream_key, extent, deviation, bound, pieces, heavy, kind=jnp.bfloat16):
    result = deviation * jax.random.normal(stream_key, extent, jnp.float32)
    if pieces:
        result = result * levels(stream_key, extent, pieces, -0.22, 0.18)
    return jnp.clip(with_spikes(result, jax.random.fold_in(stream_key, 3), *heavy), -bound, bound).astype(kind)


def setup_inputs(seed: int = 0) -> dict:
    seeds = jax.random.split(jax.random.key(seed), 8)
    return {
        "hidden_in": gaussian_with(seeds[0], (TILES, TH, TW, D), 1.0, 16.0, ((0, 64), (1, 4)), (0, 3, 64, 4.0)),
        "queries": draw_queries(jax.random.fold_in(seeds[7], 71), 0),
        "keys": draw_keys(jax.random.fold_in(seeds[7], 71), 0),
        "values": gaussian(seeds[3], (TILES, TH, TW, D), 1.0, 6.0, ((0, 64), (3, 4))),
        "w_qkv": gaussian(seeds[4], (D, 3, D), D ** -0.5, 0.1875, ((2, 4),)),
        "w_out": gaussian(seeds[5], (D, D), D ** -0.5, 0.1875, ((0, 4),)),
        "out_grad": gaussian_with(seeds[6], (TILES, TH, TW, D), 1.0, 16.0, ((0, 64), (1, 4)), (0, 3, 64, 4.0)),
    }


def settle(x):
    return lax.optimization_barrier(x.astype(jnp.bfloat16))


def window(source, start, rows, cols, span):
    band = source[start:start + rows]
    return jnp.stack([band[:, b:b + cols] for b in range(span)])


def neighbour_pass(query, pair_pad, grad_attn, row_ok, col_ok, scale):
    rows, cols = query.shape[0], query.shape[1]
    span = row_ok.shape[0]
    query32 = query.astype(jnp.float32)
    grad32 = grad_attn.astype(jnp.float32)
    score_list = []
    for a in range(span):
        near = window(pair_pad[0], a, rows, cols, span).astype(jnp.float32)
        score = jnp.einsum("rche,brche->brch", query32, near) * scale
        valid = row_ok[a][None, :, None, None] & col_ok[:, None, :, None]
        score_list.append(jnp.where(valid, score, -jnp.inf))
    scores = jnp.stack(score_list)
    top = jnp.max(scores, axis=(0, 1))
    expo = jnp.exp(scores - top)
    probs = expo / jnp.sum(expo, axis=(0, 1))
    probs16 = settle(probs).astype(jnp.float32)
    total = jnp.zeros(query.shape, jnp.float32)
    for a in range(span):
        near = window(pair_pad[1], a, rows, cols, span).astype(jnp.float32)
        total = total + jnp.einsum("brch,brche->rche", probs16[a], near)
    attn = settle(total)
    delta = jnp.einsum("rche,rche->rch", grad32, attn.astype(jnp.float32))
    grad_q = jnp.zeros(query.shape, jnp.float32)
    grad_pad = jnp.zeros(pair_pad.shape, jnp.float32)
    for a in range(span):
        near_k = window(pair_pad[0], a, rows, cols, span).astype(jnp.float32)
        near_v = window(pair_pad[1], a, rows, cols, span).astype(jnp.float32)
        dprob = jnp.einsum("rche,brche->brch", grad32, near_v)
        dscore = settle(probs[a] * (dprob - delta)).astype(jnp.float32)
        grad_q = grad_q + jnp.einsum("brch,brche->rche", dscore, near_k)
        dkey = jnp.einsum("brch,rche->brche", dscore, query32) * scale
        dval = jnp.einsum("brch,rche->brche", probs16[a], grad32)
        key_band = sum(jnp.pad(dkey[b], ((0, 0), (b, span - 1 - b), (0, 0), (0, 0))) for b in range(span))
        val_band = sum(jnp.pad(dval[b], ((0, 0), (b, span - 1 - b), (0, 0), (0, 0))) for b in range(span))
        grad_pad = grad_pad.at[0, a:a + rows].add(key_band)
        grad_pad = grad_pad.at[1, a:a + rows].add(val_band)
    return attn, (grad_q * scale).astype(jnp.bfloat16), grad_pad


def to_image(x):
    return x.reshape(TILE_ROWS, TILE_COLS, TH, TW, -1).transpose(0, 2, 1, 3, 4).reshape(IMG_H, IMG_W, -1)


def to_tiles(x):
    return x.reshape(TILE_ROWS, TH, TILE_COLS, TW, -1).transpose(0, 2, 1, 3, 4).reshape(TILES, TH, TW, -1)


def by_head(x):
    return x.reshape(IMG_H, IMG_W, HEADS, 1, HD).transpose(2, 0, 1, 3, 4)


def from_head(x):
    return x.transpose(1, 2, 0, 3, 4).reshape(IMG_H, IMG_W, D)


def reference(hidden_in, queries, keys, values, w_qkv, w_out, out_grad):
    depth = WIN // 2
    scale = HD ** -0.5
    tokens = TILES * TH * TW
    grad_flat = out_grad.reshape(tokens, D)
    grad_attn = jnp.dot(grad_flat, w_out.T, preferred_element_type=jnp.float32).astype(jnp.bfloat16)
    offsets = jnp.arange(WIN) - depth
    row_pos = jnp.arange(IMG_H)[None, :] + offsets[:, None]
    col_pos = jnp.arange(IMG_W)[None, :] + offsets[:, None]
    row_ok = (row_pos >= 0) & (row_pos < IMG_H)
    col_ok = (col_pos >= 0) & (col_pos < IMG_W)

    def per_head(items):
        query, key_h, value_h, grad_h = items
        pair = jnp.stack([key_h, value_h])
        pair_pad = jnp.pad(pair, ((0, 0), (depth, depth), (depth, depth), (0, 0), (0, 0)))
        attn, grad_q, grad_pad = neighbour_pass(query, pair_pad, grad_h, row_ok, col_ok, scale)
        inner = grad_pad[:, depth:depth + IMG_H, depth:depth + IMG_W].astype(jnp.bfloat16)
        return attn, grad_q, inner[0], inner[1]

    heads_in = (by_head(to_image(queries)), by_head(to_image(keys)), by_head(to_image(values)),
                by_head(to_image(grad_attn.reshape(TILES, TH, TW, D))))
    attn_h, grad_q_h, grad_k_h, grad_v_h = lax.map(per_head, heads_in)
    attn = to_tiles(from_head(attn_h)).reshape(tokens, D)
    grad_q = to_tiles(from_head(grad_q_h))
    grad_k = to_tiles(from_head(grad_k_h))
    grad_v = to_tiles(from_head(grad_v_h))
    grad_qkv = jnp.stack([grad_q, grad_k, grad_v], axis=3).reshape(tokens, 3 * D)
    hidden_flat = hidden_in.reshape(tokens, D)
    grad_wqkv = jnp.dot(hidden_flat.T, grad_qkv, preferred_element_type=jnp.float32).reshape(D, 3, D)
    grad_wout = jnp.dot(attn.T, grad_flat, preferred_element_type=jnp.float32)
    grad_hidden = jnp.dot(grad_qkv, w_qkv.reshape(D, 3 * D).T, preferred_element_type=jnp.float32)
    grad_hidden = grad_hidden.astype(jnp.bfloat16).reshape(TILES, TH, TW, D)
    return grad_hidden, grad_wqkv, grad_wout
```

```python
import jax
import jax.numpy as jnp
from jax import lax
from jax.experimental import pallas as pl
from jax.experimental.pallas import tpu as pltpu
from jax.sharding import Mesh
from jax.sharding import PartitionSpec as P

D = 1024
HD = 64
HEADS_HERE = 4
FEAT = HD * HEADS_HERE
TH = 32
TW = 16
TOKENS = TH * TW
DEPTH = 3
IMG_H = 256
IMG_W = 128
PAD_H = TH + 2 * DEPTH
CENTER = PAD_H * TW
EDGE = DEPTH * TW
SLOTS = 4
BAND = 40 * SLOTS
BLOCKS = 4
BLK = TOKENS // BLOCKS
BLK_ROWS = TH // BLOCKS
K_MID = (BLK_ROWS + 2 * DEPTH) * TW
K_BAND = 16 * SLOTS
K_ALL = K_MID + 2 * K_BAND
Z, YH, X, YL, CORE = 8, 2, 4, 2, 2
GRID = ("z", "yh", "x")
YX = ("yh", "x")
HEAD = ("yl", "core")
F32 = jnp.float32
BF16 = jnp.bfloat16
VMEM_LIMIT = 40 * 1024 * 1024


def dot(a, b, ca, cb):
    return lax.dot_general(a, b, (((ca,), (cb,)), ((), ())), preferred_element_type=F32)


def call(body, out_shape, scratch=(), n_smem=0, n_in=0):
    specs = [pl.BlockSpec(memory_space=pltpu.SMEM)] * n_smem
    specs += [pl.BlockSpec(memory_space=pltpu.VMEM)] * (n_in - n_smem)
    outs = jax.tree.map(lambda _: pl.BlockSpec(memory_space=pltpu.VMEM), out_shape)
    return pl.pallas_call(
        body,
        out_shape=out_shape,
        in_specs=specs,
        out_specs=outs,
        scratch_shapes=list(scratch),
        compiler_params=pltpu.CompilerParams(vmem_limit_bytes=VMEM_LIMIT),
    )


def shaped(shape, dtype=BF16):
    return jax.ShapeDtypeStruct(shape, dtype)


def pick(first_col, token_axis):
    shape = (CENTER, BAND) if token_axis == 0 else (BAND, CENTER)
    token = lax.broadcasted_iota(jnp.int32, shape, token_axis)
    slot = lax.broadcasted_iota(jnp.int32, shape, 1 - token_axis)
    lane = slot & (SLOTS - 1)
    wanted = (slot // SLOTS) * TW + first_col + lane
    return jnp.where((token == wanted) & (lane < DEPTH), 1.0, 0.0).astype(BF16)


def bands_kernel(k, v, above, below, to_left, to_right):
    left = pick(0, 1)
    right = pick(TW - DEPTH, 1)
    for i, own in enumerate((k, v)):
        mid = jnp.concatenate([above[i], own[...], below[i]], axis=0)
        to_left[i] = dot(left, mid, 1, 0).astype(BF16)
        to_right[i] = dot(right, mid, 1, 0).astype(BF16)


def stacked(x):
    lane = lax.broadcasted_iota(jnp.int32, x.shape, 1) // HD
    zero = jnp.zeros_like(x)
    return jnp.concatenate([jnp.where(lane == h, x, zero) for h in range(HEADS_HERE)], axis=0)


def unstacked(x):
    lane = lax.broadcasted_iota(jnp.int32, (BLK, FEAT), 1) // HD
    out = x[:BLK]
    for h in range(1, HEADS_HERE):
        out = jnp.where(lane == h, x[h * BLK : (h + 1) * BLK], out)
    return out


def attention_kernel(
    place, q, og0, og1, og2, og3, w_out, k, v, above, below, from_left, from_right,
    attn_out, grad_q, grad_mid, band_left, band_right,
    mid, ga, gl, gr,
):
    head = place[0]
    tile_row = place[1]
    tile_col = place[2]
    for i, own in enumerate((k, v)):
        mid[i, :EDGE] = above[i]
        mid[i, EDGE : EDGE + TOKENS] = own[...]
        mid[i, EDGE + TOKENS :] = below[i]
    for i, piece in enumerate((og0, og1, og2, og3)):
        at = pl.multiple_of((head ^ i) * BLK, BLK)
        ga[pl.ds(at, BLK), :] = dot(piece[...], w_out[...], 1, 1).astype(BF16)
    grad_mid[...] = jnp.zeros_like(grad_mid)
    gl[...] = jnp.zeros_like(gl)
    gr[...] = jnp.zeros_like(gr)

    key = lax.broadcasted_iota(jnp.int32, (1, K_ALL), 1)
    in_mid = key < K_MID
    in_left = key < K_MID + K_BAND
    slot = key & (SLOTS - 1)
    key_row = jnp.where(
        in_mid,
        key // TW,
        jnp.where(in_left, (key - K_MID) // SLOTS, (key - K_MID - K_BAND) // SLOTS),
    )
    band_col = jnp.where(in_left, slot, TW + DEPTH + slot)
    key_col = jnp.where(in_mid, (key & (TW - 1)) + DEPTH, jnp.where(slot < DEPTH, band_col, 1000))
    col_image = tile_col * TW + key_col - DEPTH
    key_col = jnp.where((col_image >= 0) & (col_image < IMG_W), key_col, 1000)
    token = lax.broadcasted_iota(jnp.int32, (BLK, 1), 0)
    row_off = key_row - token // TW
    col_off = key_col - (token & (TW - 1))
    near = (row_off >= 0) & (row_off < 7) & (col_off >= 0) & (col_off < 7)
    row_image = tile_row * TH + key_row - DEPTH

    for b in range(BLOCKS):
        row_here = row_image + b * BLK_ROWS
        valid = near & (row_here >= 0) & (row_here < IMG_H)
        bias = jnp.where(valid, 0.0, -jnp.inf).astype(F32)
        rows = slice(b * BLK, (b + 1) * BLK)
        m_rows = slice(b * BLK, b * BLK + K_MID)
        b_rows = slice(b * BLK_ROWS * SLOTS, b * BLK_ROWS * SLOTS + K_BAND)
        kk = jnp.concatenate([mid[0, m_rows], from_left[0, b_rows], from_right[0, b_rows]], axis=0)
        vv = jnp.concatenate([mid[1, m_rows], from_left[1, b_rows], from_right[1, b_rows]], axis=0)
        qs = stacked(q[rows, :] * jnp.asarray(HD**-0.5, BF16))
        gs = stacked(ga[rows, :])
        s = dot(qs, kk, 1, 1).reshape(HEADS_HERE, BLK, K_ALL) + bias[None]
        s = s.reshape(HEADS_HERE * BLK, K_ALL)
        e = jnp.exp(s - jnp.max(s, axis=1, keepdims=True))
        p = e * (1.0 / jnp.sum(e, axis=1, keepdims=True))
        p16 = p.astype(BF16)
        attn = dot(p16, vv, 1, 0).astype(BF16)
        attn_out[rows, :] = unstacked(attn)
        delta = jnp.sum(gs.astype(F32) * attn.astype(F32), axis=1, keepdims=True)
        ds = (p * (dot(gs, vv, 1, 1) - delta)).astype(BF16)
        grad_q[rows, :] = unstacked(dot(ds, kk, 1, 0) * (HD**-0.5)).astype(BF16)
        for i, g in enumerate((dot(ds, qs, 0, 0), dot(p16, gs, 0, 0))):
            grad_mid[i, m_rows] += g[:K_MID]
            gl[i, b_rows] += g[K_MID : K_MID + K_BAND]
            gr[i, b_rows] += g[K_MID + K_BAND :]
    band_left[...] = gl[...].astype(BF16)
    band_right[...] = gr[...].astype(BF16)


def put_term(out, cols, term):
    term = term.astype(BF16)
    for yx in range(YH * X):
        for z in range(Z):
            at = (z * YH * X + yx) * 16
            out[yx, z, :, cols] = term[at : at + 16]


def first_terms_kernel(place, hidden, grad_q, og0, og1, og2, og3, attn, out, og):
    head = place[0]
    for i, piece in enumerate((og0, og1, og2, og3)):
        og[pl.ds(pl.multiple_of((head ^ i) * BLK, BLK), BLK), :] = piece[...]
    put_term(out, slice(0, FEAT), dot(hidden[...], grad_q[...], 0, 0))
    put_term(out, slice(FEAT, 2 * FEAT), dot(og[...], attn[...], 0, 0))


def columns_kernel(grad_mid, from_left, from_right, inner, to_above, to_below):
    left = pick(0, 0)
    right = pick(TW - DEPTH, 0)
    for i in range(2):
        g = grad_mid[i] + dot(left, from_left[i], 1, 0) + dot(right, from_right[i], 1, 0)
        to_above[i] = g[:EDGE].astype(BF16)
        inner[i] = g[EDGE : EDGE + TOKENS]
        to_below[i] = g[EDGE + TOKENS :].astype(BF16)


def second_terms_kernel(
    place, inner, from_above, from_below, grad_q, hidden, w_qkv, terms, keep, send, grads
):
    core = place[3]
    grads[0] = grad_q[...]
    for i in range(2):
        grads[1 + i, :EDGE] = (inner[i, :EDGE] + from_above[i].astype(F32)).astype(BF16)
        grads[1 + i, EDGE : TOKENS - EDGE] = inner[i, EDGE : TOKENS - EDGE].astype(BF16)
        last = inner[i, TOKENS - EDGE :] + from_below[i].astype(F32)
        grads[1 + i, TOKENS - EDGE :] = last.astype(BF16)
    for yl in range(YL):
        for out, c in ((send, 1 - core), (keep, core)):
            at = pl.ds(pl.multiple_of((yl * CORE + c) * BLK, BLK), BLK)
            total = dot(grads[0, at, :], w_qkv[0], 1, 1)
            for j in (1, 2):
                total += dot(grads[j, at, :], w_qkv[j], 1, 1)
            out[yl] = total.astype(BF16)
    for i in range(2):
        put_term(terms, slice(i * FEAT, (i + 1) * FEAT), dot(hidden[...], grads[1 + i], 0, 0))


def halve_kernel(place, keep, got, stay, send):
    yl = place[4]
    stay[...] = keep[yl].astype(F32) + got[yl].astype(F32)
    send[...] = (keep[1 - yl].astype(F32) + got[1 - yl].astype(F32)).astype(BF16)


def add_terms_kernel(first, second, out):
    for i, terms in enumerate((first, second)):
        total = terms[0].astype(F32)
        for yx in range(1, YH * X):
            total += terms[yx].astype(F32)
        out[:, :, i * 2 * FEAT : (i + 1) * 2 * FEAT] = total.astype(BF16)


def ring(size, step):
    return [(i, (i + step) % size) for i in range(size)]


SWAP = [(0, 1), (1, 0)]


def per_device(hidden_in, queries, keys, values, w_qkv, w_out, out_grad):
    yl = lax.axis_index("yl")
    core = lax.axis_index("core")
    place = jnp.stack(
        [yl * CORE + core, lax.axis_index("z"), lax.axis_index(YX), core, yl]
    ).astype(jnp.int32)
    q = queries.reshape(TOKENS, FEAT)
    k = keys.reshape(TOKENS, FEAT)
    v = values.reshape(TOKENS, FEAT)
    w3 = w_qkv.transpose(1, 0, 2)

    og0 = out_grad.reshape(BLK, D)
    og2 = lax.ppermute(og0, "yl", SWAP)
    og1 = lax.ppermute(og0, "core", SWAP)
    og3 = lax.ppermute(og2, "core", SWAP)
    pieces = (og0, og1, og2, og3)

    below = lax.ppermute(jnp.stack([k[:EDGE], v[:EDGE]]), "z", ring(Z, -1))
    above = lax.ppermute(jnp.stack([k[-EDGE:], v[-EDGE:]]), "z", ring(Z, 1))
    band = shaped((2, BAND, FEAT))
    to_left, to_right = call(bands_kernel, (band, band), n_in=4)(k, v, above, below)
    from_right = lax.ppermute(to_left, YX, ring(YH * X, -1))
    from_left = lax.ppermute(to_right, YX, ring(YH * X, 1))
    hidden = lax.all_gather(hidden_in, HEAD, axis=1, tiled=True).reshape(TOKENS, D)

    flat = shaped((TOKENS, FEAT))
    attn, grad_q, grad_mid, band_left, band_right = call(
        attention_kernel,
        (flat, flat, shaped((2, CENTER, FEAT), F32), band, band),
        scratch=[
            pltpu.VMEM((2, CENTER, FEAT), BF16),
            pltpu.VMEM((TOKENS, FEAT), BF16),
            pltpu.VMEM((2, BAND, FEAT), F32),
            pltpu.VMEM((2, BAND, FEAT), F32),
        ],
        n_smem=1,
        n_in=13,
    )(place, q, *pieces, w_out, k, v, above, below, from_left, from_right)

    got_right = lax.ppermute(band_left, YX, ring(YH * X, -1))
    got_left = lax.ppermute(band_right, YX, ring(YH * X, 1))
    terms = shaped((YH * X, Z, 16, 2 * FEAT))
    first = call(
        first_terms_kernel, terms, scratch=[pltpu.VMEM((TOKENS, D), BF16)], n_smem=1, n_in=8
    )(place, hidden, grad_q, *pieces, attn)
    edge = shaped((2, EDGE, FEAT))
    inner, to_above, to_below = call(
        columns_kernel, (shaped((2, TOKENS, FEAT), F32), edge, edge), n_in=3
    )(grad_mid, got_left, got_right)
    got_below = lax.ppermute(to_above, "z", ring(Z, -1))
    got_above = lax.ppermute(to_below, "z", ring(Z, 1))
    first, inner = lax.optimization_barrier((first, inner))
    first = lax.all_to_all(first, YX, 0, 0, tiled=True)

    half = shaped((YL, BLK, D))
    second, keep, send = call(
        second_terms_kernel,
        (terms, half, half),
        scratch=[pltpu.VMEM((3, TOKENS, FEAT), BF16)],
        n_smem=1,
        n_in=7,
    )(place, inner, got_above, got_below, grad_q, hidden, w3)
    got = lax.ppermute(send, "core", SWAP)
    stay, send = call(halve_kernel, (shaped((BLK, D), F32), shaped((BLK, D))), n_smem=1, n_in=3)(
        place, keep, got
    )
    got = lax.ppermute(send, "yl", SWAP)
    second, stay = lax.optimization_barrier((second, stay))
    second = lax.all_to_all(second, YX, 0, 0, tiled=True)
    grad_hidden = (stay + got.astype(F32)).astype(BF16).reshape(1, 8, TW, D)

    partial = call(add_terms_kernel, shaped((Z, 16, 4 * FEAT)), n_in=2)(first, second)
    partial = lax.all_to_all(partial, "z", 0, 0, tiled=True)
    total = jnp.sum(partial.astype(F32), axis=0)
    grad_wout = total[:, FEAT : 2 * FEAT].T
    grad_wqkv = jnp.stack(
        [total[:, :FEAT], total[:, 2 * FEAT : 3 * FEAT], total[:, 3 * FEAT :]], axis=1
    )
    return grad_hidden, grad_wqkv, grad_wout


def solution(mesh):
    fine = Mesh(mesh.devices.reshape(Z, YH, X, YL, CORE), GRID + HEAD)
    return jax.shard_map(
        per_device,
        mesh=fine,
        in_specs=(
            P(GRID, HEAD, None, None),
            P(GRID, None, None, HEAD),
            P(GRID, None, None, HEAD),
            P(GRID, None, None, HEAD),
            P(None, None, HEAD),
            P(HEAD, None),
            P(GRID, HEAD, None, None),
        ),
        out_specs=(P(GRID, HEAD, None, None), P(GRID, None, HEAD), P(HEAD, GRID)),
        check_vma=False,
    )
```

```python
import jax
import jax.numpy as jnp
from jax import lax
from jax.experimental import pallas as pl
from jax.experimental.pallas import tpu as pltpu
from jax.sharding import Mesh
from jax.sharding import PartitionSpec as P

D = 1024
HD = 64
HEADS_HERE = 4
FEAT = HD * HEADS_HERE
TH = 32
TW = 16
TOKENS = TH * TW
DEPTH = 3
IMG_H = 256
IMG_W = 128
PAD_H = TH + 2 * DEPTH
CENTER = PAD_H * TW
EDGE = DEPTH * TW
SLOTS = 4
BAND = 40 * SLOTS
BLOCKS = 4
BLK = TOKENS // BLOCKS
BLK_ROWS = TH // BLOCKS
K_MID = (BLK_ROWS + 2 * DEPTH) * TW
K_BAND = 16 * SLOTS
K_ALL = K_MID + 2 * K_BAND
Z, YH, X, YL, CORE = 8, 2, 4, 2, 2
GRID = ("z", "yh", "x")
YX = ("yh", "x")
HEAD = ("yl", "core")
F32 = jnp.float32
BF16 = jnp.bfloat16
VMEM_LIMIT = 24 * 1024 * 1024


def dot(a, b, ca, cb):
    return lax.dot_general(a, b, (((ca,), (cb,)), ((), ())), preferred_element_type=F32)


def call(body, out_shape, scratch=(), n_in=0, hbm=(), hbm_out=(), flops=0):
    specs = [pl.BlockSpec(memory_space=pltpu.HBM if i in hbm else pltpu.VMEM) for i in range(n_in)]
    outs = [
        pl.BlockSpec(memory_space=pltpu.HBM if i in hbm_out else pltpu.VMEM)
        for i in range(len(out_shape))
    ]
    out_shape = [
        pltpu.HBM(o.shape, o.dtype) if i in hbm_out else o for i, o in enumerate(out_shape)
    ]
    run = pl.pallas_call(
        body,
        out_shape=out_shape,
        in_specs=specs,
        out_specs=outs,
        scratch_shapes=list(scratch),
        compiler_params=pltpu.CompilerParams(vmem_limit_bytes=VMEM_LIMIT),
        cost_estimate=pl.CostEstimate(flops=flops, bytes_accessed=0, transcendentals=0),
    )

    def on(*args):
        hold = pltpu.with_memory_space_constraint
        return run(*(hold(a, pltpu.HBM) if i in hbm else a for i, a in enumerate(args)))

    return on


def head_index():
    return lax.axis_index("yl") * CORE + lax.axis_index("core")


def shaped(shape, dtype=BF16):
    return jax.ShapeDtypeStruct(shape, dtype)


def pick(first_col, token_axis):
    shape = (CENTER, BAND) if token_axis == 0 else (BAND, CENTER)
    token = lax.broadcasted_iota(jnp.int32, shape, token_axis)
    slot = lax.broadcasted_iota(jnp.int32, shape, 1 - token_axis)
    lane = slot & (SLOTS - 1)
    wanted = (slot // SLOTS) * TW + first_col + lane
    return jnp.where((token == wanted) & (lane < DEPTH), 1.0, 0.0).astype(BF16)


def load_kernel(
    q, k, v, w_out, out_grad, hidden,
    q_out, kv, w_out_out, own_grad, own_hidden, to_above, to_below, sems,
):
    first, last = pl.ds(0, EDGE), pl.ds(TOKENS - EDGE, EDGE)
    pairs = [(k.at[first], to_above.at[0]), (v.at[first], to_above.at[1])]
    pairs += [(k.at[last], to_below.at[0]), (v.at[last], to_below.at[1])]
    pairs += [(out_grad, own_grad), (hidden, own_hidden)]
    pairs += [(k, kv.at[0]), (v, kv.at[1]), (q, q_out), (w_out, w_out_out)]
    copies = [pltpu.make_async_copy(a, b, sems.at[i]) for i, (a, b) in enumerate(pairs)]
    for copy in copies:
        copy.start()
    for copy in copies:
        copy.wait()


def bands_kernel(kv, above, below, mid, to_left, to_right):
    left = pick(0, 1)
    right = pick(TW - DEPTH, 1)
    for i in range(2):
        mid[i, :EDGE] = above[i]
        mid[i, EDGE : EDGE + TOKENS] = kv[i]
        mid[i, EDGE + TOKENS :] = below[i]
        to_left[i] = dot(left, mid[i], 1, 0).astype(BF16)
        to_right[i] = dot(right, mid[i], 1, 0).astype(BF16)


def stacked(x):
    lane = lax.broadcasted_iota(jnp.int32, x.shape, 1) // HD
    zero = jnp.zeros_like(x)
    return jnp.concatenate([jnp.where(lane == h, x, zero) for h in range(HEADS_HERE)], axis=0)


def unstacked(x):
    lane = lax.broadcasted_iota(jnp.int32, (BLK, FEAT), 1) // HD
    out = x[:BLK]
    for h in range(1, HEADS_HERE):
        out = jnp.where(lane == h, x[h * BLK : (h + 1) * BLK], out)
    return out


def attention_kernel(
    q, og0, og1, og2, og3, w_out, mid, from_left, from_right,
    attn_out, grad_q, grad_mid, band_left, band_right,
    ga, gl, gr,
):
    head = head_index()
    tile_row = lax.axis_index("z")
    tile_col = lax.axis_index("yh") * X + lax.axis_index("x")
    for i, piece in enumerate((og0, og1, og2, og3)):
        at = pl.multiple_of((head ^ i) * BLK, BLK)
        ga[pl.ds(at, BLK), :] = dot(piece[...], w_out[...], 1, 1).astype(BF16)
    grad_mid[...] = jnp.zeros_like(grad_mid)
    gl[...] = jnp.zeros_like(gl)
    gr[...] = jnp.zeros_like(gr)

    key = lax.broadcasted_iota(jnp.int32, (1, K_ALL), 1)
    in_mid = key < K_MID
    in_left = key < K_MID + K_BAND
    slot = key & (SLOTS - 1)
    key_row = jnp.where(
        in_mid,
        key // TW,
        jnp.where(in_left, (key - K_MID) // SLOTS, (key - K_MID - K_BAND) // SLOTS),
    )
    band_col = jnp.where(in_left, slot, TW + DEPTH + slot)
    key_col = jnp.where(in_mid, (key & (TW - 1)) + DEPTH, jnp.where(slot < DEPTH, band_col, 1000))
    col_image = tile_col * TW + key_col - DEPTH
    key_col = jnp.where((col_image >= 0) & (col_image < IMG_W), key_col, 1000)
    token = lax.broadcasted_iota(jnp.int32, (BLK, 1), 0)
    row_off = key_row - token // TW
    col_off = key_col - (token & (TW - 1))
    near = (row_off >= 0) & (row_off < 7) & (col_off >= 0) & (col_off < 7)
    row_image = tile_row * TH + key_row - DEPTH

    for b in range(BLOCKS):
        row_here = row_image + b * BLK_ROWS
        valid = near & (row_here >= 0) & (row_here < IMG_H)
        bias = jnp.where(valid, 0.0, -jnp.inf).astype(F32)
        rows = slice(b * BLK, (b + 1) * BLK)
        m_rows = slice(b * BLK, b * BLK + K_MID)
        b_rows = slice(b * BLK_ROWS * SLOTS, b * BLK_ROWS * SLOTS + K_BAND)
        kk = jnp.concatenate([mid[0, m_rows], from_left[0, b_rows], from_right[0, b_rows]], axis=0)
        vv = jnp.concatenate([mid[1, m_rows], from_left[1, b_rows], from_right[1, b_rows]], axis=0)
        qs = stacked(q[rows, :] * jnp.asarray(HD**-0.5, BF16))
        gs = stacked(ga[rows, :])
        s = dot(qs, kk, 1, 1).reshape(HEADS_HERE, BLK, K_ALL) + bias[None]
        s = s.reshape(HEADS_HERE * BLK, K_ALL)
        e = jnp.exp(s - jnp.max(s, axis=1, keepdims=True))
        p = e * (1.0 / jnp.sum(e, axis=1, keepdims=True))
        p16 = p.astype(BF16)
        attn = dot(p16, vv, 1, 0).astype(BF16)
        attn_out[rows, :] = unstacked(attn)
        delta = jnp.sum(gs.astype(F32) * attn.astype(F32), axis=1, keepdims=True)
        ds = (p * (dot(gs, vv, 1, 1) - delta)).astype(BF16)
        grad_q[rows, :] = unstacked(dot(ds, kk, 1, 0) * (HD**-0.5)).astype(BF16)
        for i, g in enumerate((dot(ds, qs, 0, 0), dot(p16, gs, 0, 0))):
            grad_mid[i, m_rows] += g[:K_MID]
            gl[i, b_rows] += g[K_MID : K_MID + K_BAND]
            gr[i, b_rows] += g[K_MID + K_BAND :]
    band_left[...] = gl[...].astype(BF16)
    band_right[...] = gr[...].astype(BF16)


def put_term(out, term):
    term = term.astype(BF16)
    for yx in range(YH * X):
        for z in range(Z):
            at = (z * YH * X + yx) * 16
            out[yx, z] = term[at : at + 16]


def first_terms_kernel(
    grad_q, attn, g0, g1, g2, g3, h0, h1, h2, h3, out, hidden_out, hidden, og, terms, sems
):
    head = head_index()
    for i, (g, h) in enumerate(((g0, h0), (g1, h1), (g2, h2), (g3, h3))):
        at = pl.ds(pl.multiple_of((head ^ i) * BLK, BLK), BLK)
        og[at, :] = g[...]
        hidden[at, :] = h[...]
    copies = [pltpu.make_async_copy(hidden, hidden_out, sems.at[0])]
    copies[0].start()
    for i, (left, right) in enumerate(((hidden, grad_q), (og, attn))):
        put_term(terms.at[i], dot(left[...], right[...], 0, 0))
        copies.append(pltpu.make_async_copy(terms.at[i], out.at[i], sems.at[1 + i]))
        copies[-1].start()
    for copy in copies:
        copy.wait()


def columns_kernel(grad_mid, from_left, from_right, inner, to_above, to_below):
    left = pick(0, 0)
    right = pick(TW - DEPTH, 0)
    for i in range(2):
        g = grad_mid[i] + dot(left, from_left[i], 1, 0) + dot(right, from_right[i], 1, 0)
        to_above[i] = g[:EDGE].astype(BF16)
        inner[i] = g[EDGE : EDGE + TOKENS]
        to_below[i] = g[EDGE + TOKENS :].astype(BF16)


def second_terms_kernel(
    inner, from_above, from_below, first, hidden_in, terms, grads, hidden, sems
):
    copies = [pltpu.make_async_copy(hidden_in, hidden, sems.at[0])]
    for i in range(2):
        copies.append(pltpu.make_async_copy(first.at[i], terms.at[:, i], sems.at[1 + i]))
    for copy in copies:
        copy.start()
    for i in range(2):
        grads[i, :EDGE] = (inner[i, :EDGE] + from_above[i].astype(F32)).astype(BF16)
        grads[i, EDGE : TOKENS - EDGE] = inner[i, EDGE : TOKENS - EDGE].astype(BF16)
        last = inner[i, TOKENS - EDGE :] + from_below[i].astype(F32)
        grads[i, TOKENS - EDGE :] = last.astype(BF16)
    copies[0].wait()
    for i in range(2):
        put_term(terms.at[:, 2 + i], dot(hidden[...], grads[i], 0, 0))
    copies[1].wait()
    copies[2].wait()


def hidden_grad_kernel(grad_q, grads, w_qkv, keep, send):
    core = lax.axis_index("core")
    for yl in range(YL):
        for out, c in ((send, 1 - core), (keep, core)):
            at = pl.ds(pl.multiple_of((yl * CORE + c) * BLK, BLK), BLK)
            total = dot(grad_q[at, :], w_qkv[0], 1, 1)
            for j in range(2):
                total += dot(grads[j, at, :], w_qkv[1 + j], 1, 1)
            out[yl] = total.astype(BF16)


def halve_kernel(keep, got, stay, send):
    yl = lax.axis_index("yl")
    stay[...] = keep[yl].astype(F32) + got[yl].astype(F32)
    send[...] = (keep[1 - yl].astype(F32) + got[1 - yl].astype(F32)).astype(BF16)


def summed(terms):
    total = terms[0].astype(F32)
    for i in range(1, 8):
        total += terms[i].astype(F32)
    return total


def sum_kernel(terms, out):
    for j in range(4):
        total = terms[0, j].astype(F32)
        for i in range(1, YH * X):
            total += terms[i, j].astype(F32)
        out[:, :, j * FEAT : (j + 1) * FEAT] = total.astype(BF16)


def last_kernel(parts, grad_wqkv, grad_wout):
    total = summed(parts)
    grad_wqkv[0] = total[:, :FEAT]
    grad_wout[...] = total[:, FEAT : 2 * FEAT]
    grad_wqkv[1] = total[:, 2 * FEAT : 3 * FEAT]
    grad_wqkv[2] = total[:, 3 * FEAT :]


def ring(size, step):
    return [(i, (i + step) % size) for i in range(size)]


SWAP = [(0, 1), (1, 0)]


def per_device(hidden_in, queries, keys, values, w_qkv, w_out, out_grad):
    q = queries.reshape(TOKENS, FEAT)
    k = keys.reshape(TOKENS, FEAT)
    v = values.reshape(TOKENS, FEAT)
    w3 = w_qkv.transpose(1, 0, 2)

    flat = shaped((TOKENS, FEAT))
    edge = shaped((2, EDGE, FEAT))
    band = shaped((2, BAND, FEAT))
    mids = shaped((2, CENTER, FEAT))
    own = shaped((BLK, D))
    q, kv, w_out, g0, h0, to_above, to_below = call(
        load_kernel,
        (flat, shaped((2, TOKENS, FEAT)), shaped((FEAT, D)), own, own, edge, edge),
        scratch=[pltpu.SemaphoreType.DMA((10,))],
        n_in=6,
        hbm=range(6),
    )(q, k, v, w_out, out_grad.reshape(BLK, D), hidden_in.reshape(BLK, D))

    below = lax.ppermute(to_above, "z", ring(Z, -1))
    above = lax.ppermute(to_below, "z", ring(Z, 1))
    g2 = lax.ppermute(g0, "yl", SWAP)
    g1 = lax.ppermute(g0, "core", SWAP)
    h2 = lax.ppermute(h0, "yl", SWAP)
    h1 = lax.ppermute(h0, "core", SWAP)

    mid, to_left, to_right = call(bands_kernel, (mids, band, band), n_in=3)(kv, above, below)
    from_right = lax.ppermute(to_left, YX, ring(YH * X, -1))
    from_left = lax.ppermute(to_right, YX, ring(YH * X, 1))
    g3 = lax.ppermute(g2, "core", SWAP)
    h2, _ = lax.optimization_barrier((h2, from_left))
    h3 = lax.ppermute(h2, "core", SWAP)

    attn, grad_q, grad_mid, band_left, band_right = call(
        attention_kernel,
        (flat, flat, shaped((2, CENTER, FEAT), F32), band, band),
        scratch=[
            pltpu.VMEM((TOKENS, FEAT), BF16),
            pltpu.VMEM((2, BAND, FEAT), F32),
            pltpu.VMEM((2, BAND, FEAT), F32),
        ],
        n_in=9,
    )(q, g0, g1, g2, g3, w_out, mid, from_left, from_right)

    got_right = lax.ppermute(band_left, YX, ring(YH * X, -1))
    got_left = lax.ppermute(band_right, YX, ring(YH * X, 1))
    inner, to_above, to_below = call(
        columns_kernel, (shaped((2, TOKENS, FEAT), F32), edge, edge), n_in=3
    )(grad_mid, got_left, got_right)
    got_below = lax.ppermute(to_above, "z", ring(Z, -1))
    got_above = lax.ppermute(to_below, "z", ring(Z, 1))

    first, hidden = call(
        first_terms_kernel,
        (shaped((2, YH * X, Z, 16, FEAT)), shaped((TOKENS, D))),
        scratch=[
            pltpu.VMEM((TOKENS, D), BF16),
            pltpu.VMEM((TOKENS, D), BF16),
            pltpu.VMEM((2, YH * X, Z, 16, FEAT), BF16),
            pltpu.SemaphoreType.DMA((3,)),
        ],
        n_in=10,
        hbm_out=(0, 1),
        flops=10_000_000_000,
    )(grad_q, attn, g0, g1, g2, g3, h0, h1, h2, h3)
    terms, grads = call(
        second_terms_kernel,
        (shaped((YH * X, 4, Z, 16, FEAT)), shaped((2, TOKENS, FEAT))),
        scratch=[pltpu.VMEM((TOKENS, D), BF16), pltpu.SemaphoreType.DMA((3,))],
        n_in=5,
        hbm=(3, 4),
    )(inner, got_above, got_below, first, hidden)
    terms = lax.all_to_all(terms, YX, 0, 0, tiled=True)

    half = shaped((YL, BLK, D))
    keep, send = call(hidden_grad_kernel, (half, half), n_in=3)(grad_q, grads, w3)
    got = lax.ppermute(send, "core", SWAP)
    stay, send = call(halve_kernel, (shaped((BLK, D), F32), shaped((BLK, D))), n_in=2)(keep, got)
    got = lax.ppermute(send, "yl", SWAP)
    grad_hidden = (stay + got.astype(F32)).astype(BF16).reshape(1, 8, TW, D)

    (parts,) = call(sum_kernel, (shaped((Z, 16, 4 * FEAT)),), n_in=1)(terms)
    parts = lax.all_to_all(parts, "z", 0, 0, tiled=True)
    grad_wqkv, grad_wout = call(
        last_kernel, (shaped((3, 16, FEAT), F32), shaped((16, FEAT), F32)), n_in=1
    )(parts)
    return grad_hidden, grad_wqkv.transpose(1, 0, 2), grad_wout.T


def solution(mesh):
    fine = Mesh(mesh.devices.reshape(Z, YH, X, YL, CORE), GRID + HEAD)
    return jax.shard_map(
        per_device,
        mesh=fine,
        in_specs=(
            P(GRID, HEAD, None, None),
            P(GRID, None, None, HEAD),
            P(GRID, None, None, HEAD),
            P(GRID, None, None, HEAD),
            P(None, None, HEAD),
            P(HEAD, None),
            P(GRID, HEAD, None, None),
        ),
        out_specs=(P(GRID, HEAD, None, None), P(GRID, None, HEAD), P(HEAD, GRID)),
        check_vma=False,
    )
```

```python
import jax
import jax.numpy as jnp
from jax import lax
from jax.experimental import pallas as pl
from jax.experimental.pallas import tpu as pltpu
from jax.sharding import Mesh
from jax.sharding import PartitionSpec as P

D = 1024
HD = 64
HEADS_HERE = 4
FEAT = HD * HEADS_HERE
TH = 32
TW = 16
TOKENS = TH * TW
DEPTH = 3
IMG_H = 256
IMG_W = 128
PAD_H = TH + 2 * DEPTH
CENTER = PAD_H * TW
EDGE = DEPTH * TW
SLOTS = 4
BAND = 40 * SLOTS
BLOCKS = 4
BLK = TOKENS // BLOCKS
BLK_ROWS = TH // BLOCKS
K_MID = (BLK_ROWS + 2 * DEPTH) * TW
K_BAND = 16 * SLOTS
K_ALL = K_MID + 2 * K_BAND
Z, YH, X, YL, CORE = 8, 2, 4, 2, 2
GRID = ("z", "yh", "x")
YX = ("yh", "x")
HEAD = ("yl", "core")
F32 = jnp.float32
BF16 = jnp.bfloat16
VMEM_LIMIT = 24 * 1024 * 1024


def dot(a, b, ca, cb):
    return lax.dot_general(a, b, (((ca,), (cb,)), ((), ())), preferred_element_type=F32)


def call(body, out_shape, scratch=(), n_in=0, hbm=(), hbm_out=(), flops=0, alias=None):
    specs = [pl.BlockSpec(memory_space=pltpu.HBM if i in hbm else pltpu.VMEM) for i in range(n_in)]
    outs = [
        pl.BlockSpec(memory_space=pltpu.HBM if i in hbm_out else pltpu.VMEM)
        for i in range(len(out_shape))
    ]
    out_shape = [
        pltpu.HBM(o.shape, o.dtype) if i in hbm_out else o for i, o in enumerate(out_shape)
    ]
    run = pl.pallas_call(
        body,
        out_shape=out_shape,
        in_specs=specs,
        out_specs=outs,
        scratch_shapes=list(scratch),
        input_output_aliases=alias or {},
        compiler_params=pltpu.CompilerParams(vmem_limit_bytes=VMEM_LIMIT),
        cost_estimate=pl.CostEstimate(flops=flops, bytes_accessed=0, transcendentals=0),
    )

    def on(*args):
        hold = pltpu.with_memory_space_constraint
        return run(*(hold(a, pltpu.HBM) if i in hbm else a for i, a in enumerate(args)))

    return on


def head_index():
    return lax.axis_index("yl") * CORE + lax.axis_index("core")


def shaped(shape, dtype=BF16):
    return jax.ShapeDtypeStruct(shape, dtype)


def pick(first_col, token_axis):
    shape = (CENTER, BAND) if token_axis == 0 else (BAND, CENTER)
    token = lax.broadcasted_iota(jnp.int32, shape, token_axis)
    slot = lax.broadcasted_iota(jnp.int32, shape, 1 - token_axis)
    lane = slot & (SLOTS - 1)
    wanted = (slot // SLOTS) * TW + first_col + lane
    return jnp.where((token == wanted) & (lane < DEPTH), 1.0, 0.0).astype(BF16)


def copy_all(pairs, sems):
    copies = [pltpu.make_async_copy(a, b, sems.at[i]) for i, (a, b) in enumerate(pairs)]
    for copy in copies:
        copy.start()
    for copy in copies:
        copy.wait()


def edges_kernel(k, v, to_above, to_below, sems):
    first, last = pl.ds(0, EDGE), pl.ds(TOKENS - EDGE, EDGE)
    pairs = [(k.at[first], to_above.at[0]), (v.at[first], to_above.at[1])]
    pairs += [(k.at[last], to_below.at[0]), (v.at[last], to_below.at[1])]
    copy_all(pairs, sems)


def load_kernel(
    after, q, k, v, w_out, out_grad, hidden, q_out, kv, w_out_out, own_grad, own_hidden, sems
):
    pairs = [(out_grad, own_grad), (hidden, own_hidden), (k, kv.at[0]), (v, kv.at[1])]
    copy_all(pairs + [(q, q_out), (w_out, w_out_out)], sems)


def bands_kernel(kv, above, below, mid, to_left, to_right):
    left = pick(0, 1)
    right = pick(TW - DEPTH, 1)
    for i in range(2):
        mid[i, :EDGE] = above[i]
        mid[i, EDGE : EDGE + TOKENS] = kv[i]
        mid[i, EDGE + TOKENS :] = below[i]
        to_left[i] = dot(left, mid[i], 1, 0).astype(BF16)
        to_right[i] = dot(right, mid[i], 1, 0).astype(BF16)


def stacked(x):
    lane = lax.broadcasted_iota(jnp.int32, x.shape, 1) // HD
    zero = jnp.zeros_like(x)
    return jnp.concatenate([jnp.where(lane == h, x, zero) for h in range(HEADS_HERE)], axis=0)


def unstacked(x):
    lane = lax.broadcasted_iota(jnp.int32, (BLK, FEAT), 1) // HD
    out = x[:BLK]
    for h in range(1, HEADS_HERE):
        out = jnp.where(lane == h, x[h * BLK : (h + 1) * BLK], out)
    return out


def attention_kernel(
    q, og0, og1, og2, og3, w_out, mid, from_left, from_right,
    attn_out, grad_q, grad_mid, band_left, band_right,
    ga, gl, gr,
):
    head = head_index()
    tile_row = lax.axis_index("z")
    tile_col = lax.axis_index("yh") * X + lax.axis_index("x")
    for i, piece in enumerate((og0, og1, og2, og3)):
        at = pl.multiple_of((head ^ i) * BLK, BLK)
        ga[pl.ds(at, BLK), :] = dot(piece[...], w_out[...], 1, 1).astype(BF16)
    grad_mid[...] = jnp.zeros_like(grad_mid)
    gl[...] = jnp.zeros_like(gl)
    gr[...] = jnp.zeros_like(gr)

    key = lax.broadcasted_iota(jnp.int32, (1, K_ALL), 1)
    in_mid = key < K_MID
    in_left = key < K_MID + K_BAND
    slot = key & (SLOTS - 1)
    key_row = jnp.where(
        in_mid,
        key // TW,
        jnp.where(in_left, (key - K_MID) // SLOTS, (key - K_MID - K_BAND) // SLOTS),
    )
    band_col = jnp.where(in_left, slot, TW + DEPTH + slot)
    key_col = jnp.where(in_mid, (key & (TW - 1)) + DEPTH, jnp.where(slot < DEPTH, band_col, 1000))
    col_image = tile_col * TW + key_col - DEPTH
    key_col = jnp.where((col_image >= 0) & (col_image < IMG_W), key_col, 1000)
    token = lax.broadcasted_iota(jnp.int32, (BLK, 1), 0)
    row_off = key_row - token // TW
    col_off = key_col - (token & (TW - 1))
    near = (row_off >= 0) & (row_off < 7) & (col_off >= 0) & (col_off < 7)
    row_image = tile_row * TH + key_row - DEPTH

    for b in range(BLOCKS):
        row_here = row_image + b * BLK_ROWS
        valid = near & (row_here >= 0) & (row_here < IMG_H)
        bias = jnp.where(valid, 0.0, -jnp.inf).astype(F32)
        rows = slice(b * BLK, (b + 1) * BLK)
        m_rows = slice(b * BLK, b * BLK + K_MID)
        b_rows = slice(b * BLK_ROWS * SLOTS, b * BLK_ROWS * SLOTS + K_BAND)
        kk = jnp.concatenate([mid[0, m_rows], from_left[0, b_rows], from_right[0, b_rows]], axis=0)
        vv = jnp.concatenate([mid[1, m_rows], from_left[1, b_rows], from_right[1, b_rows]], axis=0)
        qs = stacked(q[rows, :] * jnp.asarray(HD**-0.5, BF16))
        gs = stacked(ga[rows, :])
        s = dot(qs, kk, 1, 1).reshape(HEADS_HERE, BLK, K_ALL) + bias[None]
        s = s.reshape(HEADS_HERE * BLK, K_ALL)
        e = jnp.exp(s - jnp.max(s, axis=1, keepdims=True))
        p = e * (1.0 / jnp.sum(e, axis=1, keepdims=True))
        p16 = p.astype(BF16)
        attn = dot(p16, vv, 1, 0).astype(BF16)
        attn_out[rows, :] = unstacked(attn)
        delta = jnp.sum(gs.astype(F32) * attn.astype(F32), axis=1, keepdims=True)
        ds = (p * (dot(gs, vv, 1, 1) - delta)).astype(BF16)
        grad_q[rows, :] = unstacked(dot(ds, kk, 1, 0) * (HD**-0.5)).astype(BF16)
        for i, g in enumerate((dot(ds, qs, 0, 0), dot(p16, gs, 0, 0))):
            grad_mid[i, m_rows] += g[:K_MID]
            gl[i, b_rows] += g[K_MID : K_MID + K_BAND]
            gr[i, b_rows] += g[K_MID + K_BAND :]
    band_left[...] = gl[...].astype(BF16)
    band_right[...] = gr[...].astype(BF16)


def put_term(out, term):
    term = term.astype(BF16)
    for yx in range(YH * X):
        for z in range(Z):
            at = (z * YH * X + yx) * 16
            out[yx, z] = term[at : at + 16]


def hidden_kernel(after, h0, h1, h2, h3, hidden, to_above, to_below):
    head = head_index()
    for i, piece in enumerate((h0, h1, h2, h3)):
        hidden[pl.ds(pl.multiple_of((head ^ i) * BLK, BLK), BLK), :] = piece[...]
    to_above[...] = hidden[:EDGE, :]
    to_below[...] = hidden[TOKENS - EDGE :, :]


def first_terms_kernel(grad_q, attn, g0, g1, g2, g3, hidden, out, og, terms, sems):
    head = head_index()
    for i, piece in enumerate((g0, g1, g2, g3)):
        og[pl.ds(pl.multiple_of((head ^ i) * BLK, BLK), BLK), :] = piece[...]
    copies = []
    for i, (left, right) in enumerate(((hidden, grad_q), (og, attn))):
        put_term(terms.at[i], dot(left[...], right[...], 0, 0))
        copies.append(pltpu.make_async_copy(terms.at[i], out.at[:, i], sems.at[i]))
        copies[-1].start()
    for copy in copies:
        copy.wait()


def second_terms_kernel(
    grad_mid, from_left, from_right, hidden, hid_above, hid_below, first,
    out, grads, top, bottom, to_above, to_below,
    hid_mid, terms, sems,
):
    hid_mid[:EDGE] = hid_above[...]
    hid_mid[EDGE : EDGE + TOKENS] = hidden[...]
    hid_mid[EDGE + TOKENS :] = hid_below[...]
    left = pick(0, 0)
    right = pick(TW - DEPTH, 0)
    copies = []
    for i in range(2):
        g = grad_mid[i] + dot(left, from_left[i], 1, 0) + dot(right, from_right[i], 1, 0)
        g16 = g.astype(BF16)
        put_term(terms.at[i], dot(hid_mid[...], g16, 0, 0))
        copies.append(pltpu.make_async_copy(terms.at[i], out.at[:, 2 + i], sems.at[i]))
        copies[-1].start()
        to_above[i] = g16[:EDGE]
        grads[i] = g16[EDGE : EDGE + TOKENS]
        top[i] = g[EDGE : 2 * EDGE]
        bottom[i] = g[TOKENS : TOKENS + EDGE]
        to_below[i] = g16[EDGE + TOKENS :]
    for copy in copies:
        copy.wait()


def hidden_grad_kernel(
    grad_q, inner, top, bottom, from_above, from_below, w_qkv_in, keep, send, grads, w_qkv, sem
):
    copy = pltpu.make_async_copy(w_qkv_in, w_qkv, sem)
    copy.start()
    core = lax.axis_index("core")
    for i in range(2):
        grads[i, :EDGE] = (top[i] + from_above[i].astype(F32)).astype(BF16)
        grads[i, EDGE : TOKENS - EDGE] = inner[i, EDGE : TOKENS - EDGE]
        grads[i, TOKENS - EDGE :] = (bottom[i] + from_below[i].astype(F32)).astype(BF16)
    copy.wait()
    for yl in range(YL):
        for out, c in ((send, 1 - core), (keep, core)):
            at = pl.ds(pl.multiple_of((yl * CORE + c) * BLK, BLK), BLK)
            total = dot(grad_q[at, :], w_qkv[0], 1, 1)
            for j in range(2):
                total += dot(grads[j, at, :], w_qkv[1 + j], 1, 1)
            out[yl] = total.astype(BF16)


def halve_kernel(keep, got, stay, send):
    yl = lax.axis_index("yl")
    stay[...] = keep[yl].astype(F32) + got[yl].astype(F32)
    send[...] = (keep[1 - yl].astype(F32) + got[1 - yl].astype(F32)).astype(BF16)


def summed(terms):
    total = terms[0].astype(F32)
    for i in range(1, 8):
        total += terms[i].astype(F32)
    return total


def sum_kernel(terms, out):
    for j in range(4):
        total = terms[0, j].astype(F32)
        for i in range(1, YH * X):
            total += terms[i, j].astype(F32)
        out[:, :, j * FEAT : (j + 1) * FEAT] = total.astype(BF16)


def last_kernel(parts, grad_wqkv, grad_wout):
    total = summed(parts)
    grad_wqkv[0] = total[:, :FEAT]
    grad_wout[...] = total[:, FEAT : 2 * FEAT]
    grad_wqkv[1] = total[:, 2 * FEAT : 3 * FEAT]
    grad_wqkv[2] = total[:, 3 * FEAT :]


def ring(size, step):
    return [(i, (i + step) % size) for i in range(size)]


SWAP = [(0, 1), (1, 0)]
COLS = ("yh", "x", "yl")


def columns(step):
    pairs = []
    for col in range(YH * X):
        for yl in range(YL):
            to = col + step
            to_yl = yl if 0 <= to < YH * X else 1 - yl
            pairs.append((col * YL + yl, (to % (YH * X)) * YL + to_yl))
    return pairs


def per_device(hidden_in, queries, keys, values, w_qkv, w_out, out_grad):
    q = queries.reshape(TOKENS, FEAT)
    k = keys.reshape(TOKENS, FEAT)
    v = values.reshape(TOKENS, FEAT)
    w3 = w_qkv.transpose(1, 0, 2)

    flat = shaped((TOKENS, FEAT))
    edge = shaped((2, EDGE, FEAT))
    band = shaped((2, BAND, FEAT))
    mids = shaped((2, CENTER, FEAT))
    own = shaped((BLK, D))
    own_grad = out_grad.reshape(BLK, D)
    own_hidden = hidden_in.reshape(BLK, D)
    to_above, to_below = call(
        edges_kernel, (edge, edge), scratch=[pltpu.SemaphoreType.DMA((4,))], n_in=2, hbm=(0, 1)
    )(k, v)
    below = lax.ppermute(to_above, "z", ring(Z, -1))
    above = lax.ppermute(to_below, "z", ring(Z, 1))
    q, kv, w_out, g0, h0 = call(
        load_kernel,
        (flat, shaped((2, TOKENS, FEAT)), shaped((FEAT, D)), own, own),
        scratch=[pltpu.SemaphoreType.DMA((6,))],
        n_in=7,
        hbm=range(1, 7),
        flops=10_000_000_000,
    )(to_above, q, k, v, w_out, own_grad, own_hidden)
    g2 = lax.ppermute(own_grad, "yl", SWAP)
    g1 = lax.ppermute(own_grad, "core", SWAP)
    h2 = lax.ppermute(h0, "yl", SWAP)
    h1 = lax.ppermute(h0, "core", SWAP)

    mid, to_left, to_right = call(bands_kernel, (mids, band, band), n_in=3)(kv, above, below)
    from_right = lax.ppermute(to_left, COLS, columns(-1))
    from_left = lax.ppermute(to_right, COLS, columns(1))
    g2, _ = lax.optimization_barrier((g2, to_left))
    g3 = lax.ppermute(g2, "core", SWAP)
    h2, _, _ = lax.optimization_barrier((h2, from_left, from_right))
    h3 = lax.ppermute(h2, "core", SWAP)

    attn, grad_q, grad_mid, band_left, band_right = call(
        attention_kernel,
        (flat, flat, shaped((2, CENTER, FEAT), F32), band, band),
        scratch=[
            pltpu.VMEM((TOKENS, FEAT), BF16),
            pltpu.VMEM((2, BAND, FEAT), F32),
            pltpu.VMEM((2, BAND, FEAT), F32),
        ],
        n_in=9,
    )(q, g0, g1, g2, g3, w_out, mid, from_left, from_right)

    got_right = lax.ppermute(band_left, COLS, columns(-1))
    got_left = lax.ppermute(band_right, COLS, columns(1))
    hid_edge = shaped((EDGE, D))
    hidden, to_above, to_below = call(
        hidden_kernel, (shaped((TOKENS, D)), hid_edge, hid_edge), n_in=5
    )(band_left, h0, h1, h2, h3)
    hid_below = lax.ppermute(to_above, "z", ring(Z, -1))
    hid_above = lax.ppermute(to_below, "z", ring(Z, 1))
    all_terms = shaped((YH * X, 4, Z, 16, FEAT))
    (terms,) = call(
        first_terms_kernel,
        (all_terms,),
        scratch=[
            pltpu.VMEM((TOKENS, D), BF16),
            pltpu.VMEM((2, YH * X, Z, 16, FEAT), BF16),
            pltpu.SemaphoreType.DMA((2,)),
        ],
        n_in=7,
        hbm_out=(0,),
        flops=10_000_000_000,
    )(grad_q, attn, g0, g1, g2, g3, hidden)
    edge32 = shaped((2, EDGE, FEAT), F32)
    terms, grads, top, bottom, to_above, to_below = call(
        second_terms_kernel,
        (all_terms, shaped((2, TOKENS, FEAT)), edge32, edge32, edge, edge),
        scratch=[
            pltpu.VMEM((CENTER, D), BF16),
            pltpu.VMEM((2, YH * X, Z, 16, FEAT), BF16),
            pltpu.SemaphoreType.DMA((2,)),
        ],
        n_in=7,
        hbm=(6,),
        hbm_out=(0,),
        alias={6: 0},
    )(grad_mid, got_left, got_right, hidden, hid_above, hid_below, terms)
    got_below = lax.ppermute(to_above, "z", ring(Z, -1))
    got_above = lax.ppermute(to_below, "z", ring(Z, 1))
    terms = lax.all_to_all(terms, YX, 0, 0, tiled=True)

    half = shaped((YL, BLK, D))
    keep, send = call(
        hidden_grad_kernel,
        (half, half),
        scratch=[
            pltpu.VMEM((2, TOKENS, FEAT), BF16),
            pltpu.VMEM((3, D, FEAT), BF16),
            pltpu.SemaphoreType.DMA,
        ],
        n_in=7,
        hbm=(6,),
    )(grad_q, grads, top, bottom, got_above, got_below, w3)
    got = lax.ppermute(send, "core", SWAP)
    stay, send = call(halve_kernel, (shaped((BLK, D), F32), shaped((BLK, D))), n_in=2)(keep, got)
    got = lax.ppermute(send, "yl", SWAP)
    grad_hidden = (stay + got.astype(F32)).astype(BF16).reshape(1, 8, TW, D)

    (parts,) = call(sum_kernel, (shaped((Z, 16, 4 * FEAT)),), n_in=1)(terms)
    parts = lax.all_to_all(parts, "z", 0, 0, tiled=True)
    grad_wqkv, grad_wout = call(
        last_kernel, (shaped((3, 16, FEAT), F32), shaped((16, FEAT), F32)), n_in=1
    )(parts)
    return grad_hidden, grad_wqkv.transpose(1, 0, 2), grad_wout.T


def solution(mesh):
    fine = Mesh(mesh.devices.reshape(Z, YH, X, YL, CORE), GRID + HEAD)
    return jax.shard_map(
        per_device,
        mesh=fine,
        in_specs=(
            P(GRID, HEAD, None, None),
            P(GRID, None, None, HEAD),
            P(GRID, None, None, HEAD),
            P(GRID, None, None, HEAD),
            P(None, None, HEAD),
            P(HEAD, None),
            P(GRID, HEAD, None, None),
        ),
        out_specs=(P(GRID, HEAD, None, None), P(GRID, None, HEAD), P(HEAD, GRID)),
        check_vma=False,
    )
```

```python
import jax
import jax.numpy as jnp
from jax import lax
from jax.experimental import pallas as pl
from jax.experimental.pallas import tpu as pltpu
from jax.sharding import Mesh
from jax.sharding import PartitionSpec as P

D = 1024
HD = 64
HEADS_HERE = 4
FEAT = HD * HEADS_HERE
TH = 32
TW = 16
TOKENS = TH * TW
DEPTH = 3
IMG_H = 256
IMG_W = 128
PAD_H = TH + 2 * DEPTH
CENTER = PAD_H * TW
EDGE = DEPTH * TW
SLOTS = 4
BAND = 40 * SLOTS
SENT = 128
BLOCKS = 4
BLK = TOKENS // BLOCKS
BLK_ROWS = TH // BLOCKS
K_MID = (BLK_ROWS + 2 * DEPTH) * TW
K_BAND = 16 * SLOTS
K_ALL = K_MID + 2 * K_BAND
Z, YH, X, YL, CORE = 8, 2, 4, 2, 2
GRID = ("z", "yh", "x")
YX = ("yh", "x")
HEAD = ("yl", "core")
F32 = jnp.float32
BF16 = jnp.bfloat16
VMEM_LIMIT = 24 * 1024 * 1024


def dot(a, b, ca, cb):
    return lax.dot_general(a, b, (((ca,), (cb,)), ((), ())), preferred_element_type=F32)


def call(body, out_shape, scratch=(), n_in=0, hbm=(), hbm_out=(), flops=0, alias=None):
    specs = [pl.BlockSpec(memory_space=pltpu.HBM if i in hbm else pltpu.VMEM) for i in range(n_in)]
    outs = [
        pl.BlockSpec(memory_space=pltpu.HBM if i in hbm_out else pltpu.VMEM)
        for i in range(len(out_shape))
    ]
    out_shape = [
        pltpu.HBM(o.shape, o.dtype) if i in hbm_out else o for i, o in enumerate(out_shape)
    ]
    run = pl.pallas_call(
        body,
        out_shape=out_shape,
        in_specs=specs,
        out_specs=outs,
        scratch_shapes=list(scratch),
        input_output_aliases=alias or {},
        compiler_params=pltpu.CompilerParams(vmem_limit_bytes=VMEM_LIMIT),
        cost_estimate=pl.CostEstimate(flops=flops, bytes_accessed=0, transcendentals=0),
    )

    def on(*args):
        hold = pltpu.with_memory_space_constraint
        return run(*(hold(a, pltpu.HBM) if i in hbm else a for i, a in enumerate(args)))

    return on


def head_index():
    return lax.axis_index("yl") * CORE + lax.axis_index("core")


def shaped(shape, dtype=BF16):
    return jax.ShapeDtypeStruct(shape, dtype)


def pick(first_col, token_axis):
    shape = (CENTER, SENT) if token_axis == 0 else (SENT, CENTER)
    token = lax.broadcasted_iota(jnp.int32, shape, token_axis)
    sent = lax.broadcasted_iota(jnp.int32, shape, 1 - token_axis)
    row = (sent * 171) >> 9
    wanted = row * TW + first_col + sent - DEPTH * row
    return jnp.where((token == wanted) & (row < PAD_H), 1.0, 0.0).astype(BF16)


def spread(band_axis):
    shape = (BAND, SENT) if band_axis == 0 else (SENT, BAND)
    slot = lax.broadcasted_iota(jnp.int32, shape, band_axis)
    sent = lax.broadcasted_iota(jnp.int32, shape, 1 - band_axis)
    lane = slot & (SLOTS - 1)
    wanted = (slot // SLOTS) * DEPTH + lane
    return jnp.where((sent == wanted) & (lane < DEPTH) & (slot < PAD_H * SLOTS), 1.0, 0.0).astype(BF16)


def copy_all(pairs, sems):
    copies = [pltpu.make_async_copy(a, b, sems.at[i]) for i, (a, b) in enumerate(pairs)]
    for copy in copies:
        copy.start()
    for copy in copies:
        copy.wait()


def edges_kernel(k, v, to_above, to_below, sems):
    first, last = pl.ds(0, EDGE), pl.ds(TOKENS - EDGE, EDGE)
    pairs = [(k.at[first], to_above.at[0]), (v.at[first], to_above.at[1])]
    pairs += [(k.at[last], to_below.at[0]), (v.at[last], to_below.at[1])]
    copy_all(pairs, sems)


def load_kernel(
    after, q, k, v, w_out, out_grad, hidden, q_out, kv, w_out_out, own_grad, own_hidden, sems
):
    pairs = [(out_grad, own_grad), (hidden, own_hidden), (k, kv.at[0]), (v, kv.at[1])]
    copy_all(pairs + [(q, q_out), (w_out, w_out_out)], sems)


def bands_kernel(kv, above, below, mid, to_left, to_right):
    left = pick(0, 1)
    right = pick(TW - DEPTH, 1)
    for i in range(2):
        mid[i, :EDGE] = above[i]
        mid[i, EDGE : EDGE + TOKENS] = kv[i]
        mid[i, EDGE + TOKENS :] = below[i]
        to_left[i] = dot(left, mid[i], 1, 0).astype(BF16)
        to_right[i] = dot(right, mid[i], 1, 0).astype(BF16)


def stacked(x):
    lane = lax.broadcasted_iota(jnp.int32, x.shape, 1) // HD
    zero = jnp.zeros_like(x)
    return jnp.concatenate([jnp.where(lane == h, x, zero) for h in range(HEADS_HERE)], axis=0)


def unstacked(x):
    lane = lax.broadcasted_iota(jnp.int32, (BLK, FEAT), 1) // HD
    out = x[:BLK]
    for h in range(1, HEADS_HERE):
        out = jnp.where(lane == h, x[h * BLK : (h + 1) * BLK], out)
    return out


def attention_kernel(
    q, og0, og1, og2, og3, w_out, mid, sent_left, sent_right,
    attn_out, grad_q, grad_mid, band_left, band_right,
    ga, gl, gr, from_left, from_right,
):
    head = head_index()
    tile_row = lax.axis_index("z")
    tile_col = lax.axis_index("yh") * X + lax.axis_index("x")
    for i, piece in enumerate((og0, og1, og2, og3)):
        at = pl.multiple_of((head ^ i) * BLK, BLK)
        ga[pl.ds(at, BLK), :] = dot(piece[...], w_out[...], 1, 1).astype(BF16)
    spreading = spread(0)
    for i in range(2):
        from_left[i] = dot(spreading, sent_left[i], 1, 0).astype(BF16)
        from_right[i] = dot(spreading, sent_right[i], 1, 0).astype(BF16)
    grad_mid[...] = jnp.zeros_like(grad_mid)
    gl[...] = jnp.zeros_like(gl)
    gr[...] = jnp.zeros_like(gr)

    key = lax.broadcasted_iota(jnp.int32, (1, K_ALL), 1)
    in_mid = key < K_MID
    in_left = key < K_MID + K_BAND
    slot = key & (SLOTS - 1)
    key_row = jnp.where(
        in_mid,
        key // TW,
        jnp.where(in_left, (key - K_MID) // SLOTS, (key - K_MID - K_BAND) // SLOTS),
    )
    band_col = jnp.where(in_left, slot, TW + DEPTH + slot)
    key_col = jnp.where(in_mid, (key & (TW - 1)) + DEPTH, jnp.where(slot < DEPTH, band_col, 1000))
    col_image = tile_col * TW + key_col - DEPTH
    key_col = jnp.where((col_image >= 0) & (col_image < IMG_W), key_col, 1000)
    token = lax.broadcasted_iota(jnp.int32, (BLK, 1), 0)
    row_off = key_row - token // TW
    col_off = key_col - (token & (TW - 1))
    near = (row_off >= 0) & (row_off < 7) & (col_off >= 0) & (col_off < 7)
    row_image = tile_row * TH + key_row - DEPTH

    for b in range(BLOCKS):
        row_here = row_image + b * BLK_ROWS
        valid = near & (row_here >= 0) & (row_here < IMG_H)
        bias = jnp.where(valid, 0.0, -jnp.inf).astype(F32)
        rows = slice(b * BLK, (b + 1) * BLK)
        m_rows = slice(b * BLK, b * BLK + K_MID)
        b_rows = slice(b * BLK_ROWS * SLOTS, b * BLK_ROWS * SLOTS + K_BAND)
        kk = jnp.concatenate([mid[0, m_rows], from_left[0, b_rows], from_right[0, b_rows]], axis=0)
        vv = jnp.concatenate([mid[1, m_rows], from_left[1, b_rows], from_right[1, b_rows]], axis=0)
        qs = stacked(q[rows, :] * jnp.asarray(HD**-0.5, BF16))
        gs = stacked(ga[rows, :])
        s = dot(qs, kk, 1, 1).reshape(HEADS_HERE, BLK, K_ALL) + bias[None]
        s = s.reshape(HEADS_HERE * BLK, K_ALL)
        e = jnp.exp(s - jnp.max(s, axis=1, keepdims=True))
        p = e * (1.0 / jnp.sum(e, axis=1, keepdims=True))
        p16 = p.astype(BF16)
        attn = dot(p16, vv, 1, 0).astype(BF16)
        attn_out[rows, :] = unstacked(attn)
        delta = jnp.sum(gs.astype(F32) * attn.astype(F32), axis=1, keepdims=True)
        ds = (p * (dot(gs, vv, 1, 1) - delta)).astype(BF16)
        grad_q[rows, :] = unstacked(dot(ds, kk, 1, 0) * (HD**-0.5)).astype(BF16)
        for i, g in enumerate((dot(ds, qs, 0, 0), dot(p16, gs, 0, 0))):
            grad_mid[i, m_rows] += g[:K_MID]
            gl[i, b_rows] += g[K_MID : K_MID + K_BAND]
            gr[i, b_rows] += g[K_MID + K_BAND :]
    joining = spread(1)
    for i in range(2):
        band_left[i] = dot(joining, gl[i].astype(BF16), 1, 0).astype(BF16)
        band_right[i] = dot(joining, gr[i].astype(BF16), 1, 0).astype(BF16)


def put_term(out, term):
    term = term.astype(BF16)
    for yx in range(YH * X):
        for z in range(Z):
            at = (z * YH * X + yx) * 16
            out[yx, z] = term[at : at + 16]


def hidden_kernel(after, h0, h1, h2, h3, hidden, to_above, to_below):
    head = head_index()
    for i, piece in enumerate((h0, h1, h2, h3)):
        hidden[pl.ds(pl.multiple_of((head ^ i) * BLK, BLK), BLK), :] = piece[...]
    to_above[...] = hidden[:EDGE, :]
    to_below[...] = hidden[TOKENS - EDGE :, :]


def first_terms_kernel(grad_q, attn, g0, g1, g2, g3, hidden, out, og, terms, sems):
    head = head_index()
    for i, piece in enumerate((g0, g1, g2, g3)):
        og[pl.ds(pl.multiple_of((head ^ i) * BLK, BLK), BLK), :] = piece[...]
    copies = []
    for i, (left, right) in enumerate(((hidden, grad_q), (og, attn))):
        put_term(terms.at[i], dot(left[...], right[...], 0, 0))
        copies.append(pltpu.make_async_copy(terms.at[i], out.at[:, i], sems.at[i]))
        copies[-1].start()
    for copy in copies:
        copy.wait()


def second_terms_kernel(
    grad_mid, from_left, from_right, hidden, hid_above, hid_below, first,
    out, grads, top, bottom, to_above, to_below,
    hid_mid, terms, sems,
):
    hid_mid[:EDGE] = hid_above[...]
    hid_mid[EDGE : EDGE + TOKENS] = hidden[...]
    hid_mid[EDGE + TOKENS :] = hid_below[...]
    left = pick(0, 0)
    right = pick(TW - DEPTH, 0)
    copies = []
    for i in range(2):
        g = grad_mid[i] + dot(left, from_left[i], 1, 0) + dot(right, from_right[i], 1, 0)
        g16 = g.astype(BF16)
        put_term(terms.at[i], dot(hid_mid[...], g16, 0, 0))
        copies.append(pltpu.make_async_copy(terms.at[i], out.at[:, 2 + i], sems.at[i]))
        copies[-1].start()
        to_above[i] = g16[:EDGE]
        grads[i] = g16[EDGE : EDGE + TOKENS]
        top[i] = g[EDGE : 2 * EDGE]
        bottom[i] = g[TOKENS : TOKENS + EDGE]
        to_below[i] = g16[EDGE + TOKENS :]
    for copy in copies:
        copy.wait()


def hidden_grad_kernel(
    grad_q, inner, top, bottom, from_above, from_below, w_qkv_in, keep, send, grads, w_qkv, sem
):
    copy = pltpu.make_async_copy(w_qkv_in, w_qkv, sem)
    copy.start()
    core = lax.axis_index("core")
    for i in range(2):
        grads[i, :EDGE] = (top[i] + from_above[i].astype(F32)).astype(BF16)
        grads[i, EDGE : TOKENS - EDGE] = inner[i, EDGE : TOKENS - EDGE]
        grads[i, TOKENS - EDGE :] = (bottom[i] + from_below[i].astype(F32)).astype(BF16)
    copy.wait()
    for yl in range(YL):
        for out, c in ((send, 1 - core), (keep, core)):
            at = pl.ds(pl.multiple_of((yl * CORE + c) * BLK, BLK), BLK)
            total = dot(grad_q[at, :], w_qkv[0], 1, 1)
            for j in range(2):
                total += dot(grads[j, at, :], w_qkv[1 + j], 1, 1)
            out[yl] = total.astype(BF16)


def halve_kernel(keep, got, stay, send):
    yl = lax.axis_index("yl")
    stay[...] = keep[yl].astype(F32) + got[yl].astype(F32)
    send[...] = (keep[1 - yl].astype(F32) + got[1 - yl].astype(F32)).astype(BF16)


def summed(terms):
    total = terms[0].astype(F32)
    for i in range(1, 8):
        total += terms[i].astype(F32)
    return total


def sum_kernel(terms, out):
    for j in range(4):
        total = terms[0, j].astype(F32)
        for i in range(1, YH * X):
            total += terms[i, j].astype(F32)
        out[:, :, j * FEAT : (j + 1) * FEAT] = total.astype(BF16)


def last_kernel(parts, grad_wqkv, grad_wout):
    total = summed(parts)
    grad_wqkv[0] = total[:, :FEAT]
    grad_wout[...] = total[:, FEAT : 2 * FEAT]
    grad_wqkv[1] = total[:, 2 * FEAT : 3 * FEAT]
    grad_wqkv[2] = total[:, 3 * FEAT :]


def ring(size, step):
    return [(i, (i + step) % size) for i in range(size)]


SWAP = [(0, 1), (1, 0)]
COLS = ("yh", "x", "yl")


def columns(step):
    pairs = []
    for col in range(YH * X):
        for yl in range(YL):
            to = col + step
            to_yl = yl if 0 <= to < YH * X else 1 - yl
            pairs.append((col * YL + yl, (to % (YH * X)) * YL + to_yl))
    return pairs


def per_device(hidden_in, queries, keys, values, w_qkv, w_out, out_grad):
    q = queries.reshape(TOKENS, FEAT)
    k = keys.reshape(TOKENS, FEAT)
    v = values.reshape(TOKENS, FEAT)
    w3 = w_qkv.transpose(1, 0, 2)

    flat = shaped((TOKENS, FEAT))
    edge = shaped((2, EDGE, FEAT))
    band = shaped((2, SENT, FEAT))
    mids = shaped((2, CENTER, FEAT))
    own = shaped((BLK, D))
    own_grad = out_grad.reshape(BLK, D)
    own_hidden = hidden_in.reshape(BLK, D)
    to_above, to_below = call(
        edges_kernel, (edge, edge), scratch=[pltpu.SemaphoreType.DMA((4,))], n_in=2, hbm=(0, 1)
    )(k, v)
    below = lax.ppermute(to_above, "z", ring(Z, -1))
    above = lax.ppermute(to_below, "z", ring(Z, 1))
    q, kv, w_out, g0, h0 = call(
        load_kernel,
        (flat, shaped((2, TOKENS, FEAT)), shaped((FEAT, D)), own, own),
        scratch=[pltpu.SemaphoreType.DMA((6,))],
        n_in=7,
        hbm=range(1, 7),
        flops=10_000_000_000,
    )(to_above, q, k, v, w_out, own_grad, own_hidden)
    g2 = lax.ppermute(own_grad, "yl", SWAP)
    late, _ = lax.optimization_barrier((own_hidden, below))
    h2 = lax.ppermute(late, "yl", SWAP)

    mid, to_left, to_right = call(bands_kernel, (mids, band, band), n_in=3)(kv, above, below)
    from_right = lax.ppermute(to_left, COLS, columns(-1))
    from_left = lax.ppermute(to_right, COLS, columns(1))
    g2, _ = lax.optimization_barrier((g2, to_left))
    g3 = lax.ppermute(g2, "core", SWAP)
    g1 = lax.ppermute(g0, "core", SWAP)
    h1 = lax.ppermute(h0, "core", SWAP)
    h2, _, _ = lax.optimization_barrier((h2, from_left, from_right))
    h3 = lax.ppermute(h2, "core", SWAP)

    attn, grad_q, grad_mid, band_left, band_right = call(
        attention_kernel,
        (flat, flat, shaped((2, CENTER, FEAT), F32), band, band),
        scratch=[
            pltpu.VMEM((TOKENS, FEAT), BF16),
            pltpu.VMEM((2, BAND, FEAT), F32),
            pltpu.VMEM((2, BAND, FEAT), F32),
            pltpu.VMEM((2, BAND, FEAT), BF16),
            pltpu.VMEM((2, BAND, FEAT), BF16),
        ],
        n_in=9,
    )(q, g0, g1, g2, g3, w_out, mid, from_left, from_right)

    got_right = lax.ppermute(band_left, COLS, columns(-1))
    got_left = lax.ppermute(band_right, COLS, columns(1))
    hid_edge = shaped((EDGE, D))
    hidden, to_above, to_below = call(
        hidden_kernel, (shaped((TOKENS, D)), hid_edge, hid_edge), n_in=5
    )(band_left, h0, h1, h2, h3)
    hid_below = lax.ppermute(to_above, "z", ring(Z, -1))
    hid_above = lax.ppermute(to_below, "z", ring(Z, 1))
    all_terms = shaped((YH * X, 4, Z, 16, FEAT))
    (terms,) = call(
        first_terms_kernel,
        (all_terms,),
        scratch=[
            pltpu.VMEM((TOKENS, D), BF16),
            pltpu.VMEM((2, YH * X, Z, 16, FEAT), BF16),
            pltpu.SemaphoreType.DMA((2,)),
        ],
        n_in=7,
        hbm_out=(0,),
        flops=10_000_000_000,
    )(grad_q, attn, g0, g1, g2, g3, hidden)
    edge32 = shaped((2, EDGE, FEAT), F32)
    terms, grads, top, bottom, to_above, to_below = call(
        second_terms_kernel,
        (all_terms, shaped((2, TOKENS, FEAT)), edge32, edge32, edge, edge),
        scratch=[
            pltpu.VMEM((CENTER, D), BF16),
            pltpu.VMEM((2, YH * X, Z, 16, FEAT), BF16),
            pltpu.SemaphoreType.DMA((2,)),
        ],
        n_in=7,
        hbm=(6,),
        hbm_out=(0,),
        alias={6: 0},
    )(grad_mid, got_left, got_right, hidden, hid_above, hid_below, terms)
    got_below = lax.ppermute(to_above, "z", ring(Z, -1))
    got_above = lax.ppermute(to_below, "z", ring(Z, 1))
    terms = lax.all_to_all(terms, YX, 0, 0, tiled=True)

    half = shaped((YL, BLK, D))
    keep, send = call(
        hidden_grad_kernel,
        (half, half),
        scratch=[
            pltpu.VMEM((2, TOKENS, FEAT), BF16),
            pltpu.VMEM((3, D, FEAT), BF16),
            pltpu.SemaphoreType.DMA,
        ],
        n_in=7,
        hbm=(6,),
    )(grad_q, grads, top, bottom, got_above, got_below, w3)
    got = lax.ppermute(send, "core", SWAP)
    stay, send = call(halve_kernel, (shaped((BLK, D), F32), shaped((BLK, D))), n_in=2)(keep, got)
    got = lax.ppermute(send, "yl", SWAP)
    grad_hidden = (stay + got.astype(F32)).astype(BF16).reshape(1, 8, TW, D)

    (parts,) = call(sum_kernel, (shaped((Z, 16, 4 * FEAT)),), n_in=1)(terms)
    parts = lax.all_to_all(parts, "z", 0, 0, tiled=True)
    grad_wqkv, grad_wout = call(
        last_kernel, (shaped((3, 16, FEAT), F32), shaped((16, FEAT), F32)), n_in=1
    )(parts)
    return grad_hidden, grad_wqkv.transpose(1, 0, 2), grad_wout.T


def solution(mesh):
    fine = Mesh(mesh.devices.reshape(Z, YH, X, YL, CORE), GRID + HEAD)
    return jax.shard_map(
        per_device,
        mesh=fine,
        in_specs=(
            P(GRID, HEAD, None, None),
            P(GRID, None, None, HEAD),
            P(GRID, None, None, HEAD),
            P(GRID, None, None, HEAD),
            P(None, None, HEAD),
            P(HEAD, None),
            P(GRID, HEAD, None, None),
        ),
        out_specs=(P(GRID, HEAD, None, None), P(GRID, None, HEAD), P(HEAD, GRID)),
        check_vma=False,
    )
```

```python
import jax
import jax.numpy as jnp
from jax import lax
from jax.experimental import pallas as pl
from jax.experimental.pallas import tpu as pltpu
from jax.sharding import Mesh
from jax.sharding import PartitionSpec as P

D = 1024
HD = 64
HEADS_HERE = 4
FEAT = HD * HEADS_HERE
TH = 32
TW = 16
TOKENS = TH * TW
DEPTH = 3
IMG_H = 256
IMG_W = 128
PAD_H = TH + 2 * DEPTH
CENTER = PAD_H * TW
EDGE = DEPTH * TW
SLOTS = 4
BAND = 40 * SLOTS
SENT = 128
CHUNKS = 4
PIECE = TOKENS // 4
BLOCKS = 8
BLK = TOKENS // BLOCKS
BLK_ROWS = TH // BLOCKS
K_MID = (BLK_ROWS + 2 * DEPTH) * TW
K_BAND = 12 * SLOTS
K_ALL = K_MID + 2 * K_BAND
Z, YH, X, YL, CORE = 8, 2, 4, 2, 2
GRID = ("z", "yh", "x")
YX = ("yh", "x")
HEAD = ("yl", "core")
F32 = jnp.float32
BF16 = jnp.bfloat16
VMEM_LIMIT = 24 * 1024 * 1024


def dot(a, b, ca, cb):
    return lax.dot_general(a, b, (((ca,), (cb,)), ((), ())), preferred_element_type=F32)


def call(body, out_shape, scratch=(), n_in=0, hbm=(), hbm_out=(), flops=0, alias=None):
    specs = [pl.BlockSpec(memory_space=pltpu.HBM if i in hbm else pltpu.VMEM) for i in range(n_in)]
    outs = [
        pl.BlockSpec(memory_space=pltpu.HBM if i in hbm_out else pltpu.VMEM)
        for i in range(len(out_shape))
    ]
    out_shape = [
        pltpu.HBM(o.shape, o.dtype) if i in hbm_out else o for i, o in enumerate(out_shape)
    ]
    run = pl.pallas_call(
        body,
        out_shape=out_shape,
        in_specs=specs,
        out_specs=outs,
        scratch_shapes=list(scratch),
        input_output_aliases=alias or {},
        compiler_params=pltpu.CompilerParams(vmem_limit_bytes=VMEM_LIMIT),
        cost_estimate=pl.CostEstimate(flops=flops, bytes_accessed=0, transcendentals=0),
    )

    def on(*args):
        hold = pltpu.with_memory_space_constraint
        return run(*(hold(a, pltpu.HBM) if i in hbm else a for i, a in enumerate(args)))

    return on


def head_index():
    return lax.axis_index("yl") * CORE + lax.axis_index("core")


def shaped(shape, dtype=BF16):
    return jax.ShapeDtypeStruct(shape, dtype)


def pick(first_col, token_axis):
    shape = (CENTER, SENT) if token_axis == 0 else (SENT, CENTER)
    token = lax.broadcasted_iota(jnp.int32, shape, token_axis)
    sent = lax.broadcasted_iota(jnp.int32, shape, 1 - token_axis)
    row = (sent * 171) >> 9
    wanted = row * TW + first_col + sent - DEPTH * row
    return jnp.where((token == wanted) & (row < PAD_H), 1.0, 0.0).astype(BF16)


def spread(band_axis):
    shape = (BAND, SENT) if band_axis == 0 else (SENT, BAND)
    slot = lax.broadcasted_iota(jnp.int32, shape, band_axis)
    sent = lax.broadcasted_iota(jnp.int32, shape, 1 - band_axis)
    lane = slot & (SLOTS - 1)
    wanted = (slot // SLOTS) * DEPTH + lane
    return jnp.where((sent == wanted) & (lane < DEPTH) & (slot < PAD_H * SLOTS), 1.0, 0.0).astype(BF16)


def copy_all(pairs, sems):
    copies = [pltpu.make_async_copy(a, b, sems.at[i]) for i, (a, b) in enumerate(pairs)]
    for copy in copies:
        copy.start()
    for copy in copies:
        copy.wait()


def edges_kernel(k, v, to_above, to_below, sems):
    first, last = pl.ds(0, EDGE), pl.ds(TOKENS - EDGE, EDGE)
    pairs = [(k.at[first], to_above.at[0]), (v.at[first], to_above.at[1])]
    pairs += [(k.at[last], to_below.at[0]), (v.at[last], to_below.at[1])]
    copy_all(pairs, sems)


def load_kernel(
    after, q, k, v, w_out, out_grad, hidden, q_out, kv, w_out_out, own_grad, own_hidden, sems
):
    pairs = [(out_grad, own_grad), (hidden, own_hidden), (k, kv.at[0]), (v, kv.at[1])]
    copy_all(pairs + [(q, q_out), (w_out, w_out_out)], sems)


def bands_kernel(kv, above, below, mid, to_left, to_right):
    left = pick(0, 1)
    right = pick(TW - DEPTH, 1)
    for i in range(2):
        mid[i, :EDGE] = above[i]
        mid[i, EDGE : EDGE + TOKENS] = kv[i]
        mid[i, EDGE + TOKENS :] = below[i]
        to_left[i] = dot(left, mid[i], 1, 0).astype(BF16)
        to_right[i] = dot(right, mid[i], 1, 0).astype(BF16)


def stacked(x):
    lane = lax.broadcasted_iota(jnp.int32, x.shape, 1) // HD
    zero = jnp.zeros_like(x)
    return jnp.concatenate([jnp.where(lane == h, x, zero) for h in range(HEADS_HERE)], axis=0)


def unstacked(x):
    lane = lax.broadcasted_iota(jnp.int32, (BLK, FEAT), 1) // HD
    out = x[:BLK]
    for h in range(1, HEADS_HERE):
        out = jnp.where(lane == h, x[h * BLK : (h + 1) * BLK], out)
    return out


def block_of(b):
    rows = slice(b * BLK, (b + 1) * BLK)
    m_rows = slice(b * BLK, b * BLK + K_MID)
    b_rows = slice(b * BLK_ROWS * SLOTS, b * BLK_ROWS * SLOTS + K_BAND)
    return rows, m_rows, b_rows


def attention_kernel(
    q, og0, og1, og2, og3, w_out, mid, sent_left, sent_right,
    attn_out, grad_q, grad_mid, band_left, band_right,
    ga, gl, gr, from_left, from_right,
):
    head = head_index()
    tile_row = lax.axis_index("z")
    tile_col = lax.axis_index("yh") * X + lax.axis_index("x")
    for i, piece in enumerate((og0, og1, og2, og3)):
        at = pl.multiple_of((head ^ i) * PIECE, PIECE)
        ga[pl.ds(at, PIECE), :] = dot(piece[...], w_out[...], 1, 1).astype(BF16)
    spreading = spread(0)
    for i in range(2):
        from_left[i] = dot(spreading, sent_left[i], 1, 0).astype(BF16)
        from_right[i] = dot(spreading, sent_right[i], 1, 0).astype(BF16)
    grad_mid[...] = jnp.zeros_like(grad_mid)
    gl[...] = jnp.zeros_like(gl)
    gr[...] = jnp.zeros_like(gr)

    key = lax.broadcasted_iota(jnp.int32, (1, K_ALL), 1)
    in_mid = key < K_MID
    in_left = key < K_MID + K_BAND
    slot = key & (SLOTS - 1)
    key_row = jnp.where(
        in_mid,
        key // TW,
        jnp.where(in_left, (key - K_MID) // SLOTS, (key - K_MID - K_BAND) // SLOTS),
    )
    band_col = jnp.where(in_left, slot, TW + DEPTH + slot)
    key_col = jnp.where(in_mid, (key & (TW - 1)) + DEPTH, jnp.where(slot < DEPTH, band_col, 1000))
    col_image = tile_col * TW + key_col - DEPTH
    key_col = jnp.where((col_image >= 0) & (col_image < IMG_W), key_col, 1000)
    token = lax.broadcasted_iota(jnp.int32, (BLK, 1), 0)
    row_off = key_row - token // TW
    col_off = key_col - (token & (TW - 1))
    near = (row_off >= 0) & (row_off < 7) & (col_off >= 0) & (col_off < 7)
    row_image = tile_row * TH + key_row - DEPTH

    def start(b):
        rows, m_rows, b_rows = block_of(b)
        kk = jnp.concatenate([mid[0, m_rows], from_left[0, b_rows], from_right[0, b_rows]], axis=0)
        vv = jnp.concatenate([mid[1, m_rows], from_left[1, b_rows], from_right[1, b_rows]], axis=0)
        qs = stacked(q[rows, :] * jnp.asarray(HD**-0.5, BF16))
        gs = stacked(ga[rows, :])
        return kk, vv, qs, gs, dot(qs, kk, 1, 1), dot(gs, vv, 1, 1)

    def soften(b, kk, vv, qs, gs, s, dprob):
        row_here = row_image + b * BLK_ROWS
        valid = near & (row_here >= 0) & (row_here < IMG_H)
        bias = jnp.where(valid, 0.0, -jnp.inf).astype(F32)
        s = (s.reshape(HEADS_HERE, BLK, K_ALL) + bias[None]).reshape(HEADS_HERE * BLK, K_ALL)
        e = jnp.exp(s - jnp.max(s, axis=1, keepdims=True))
        p = e * (1.0 / jnp.sum(e, axis=1, keepdims=True))
        return kk, vv, qs, gs, dprob, p, p.astype(BF16)

    def apply(b, kk, vv, qs, gs, dprob, p, p16):
        return kk, qs, gs, dprob, p, dot(p16, vv, 1, 0).astype(BF16), dot(p16, gs, 0, 0)

    def finish(b, kk, qs, gs, dprob, p, attn, grad_v):
        rows, m_rows, b_rows = block_of(b)
        attn_out[rows, :] = unstacked(attn)
        delta = jnp.sum(gs.astype(F32) * attn.astype(F32), axis=1, keepdims=True)
        return kk, qs, (p * (dprob - delta)).astype(BF16), grad_v

    def spill(b, kk, qs, ds, grad_v):
        rows, m_rows, b_rows = block_of(b)
        grad_q[rows, :] = unstacked(dot(ds, kk, 1, 0) * (HD**-0.5)).astype(BF16)
        for i, g in enumerate((dot(ds, qs, 0, 0), grad_v)):
            grad_mid[i, m_rows] += g[:K_MID]
            gl[i, b_rows] += g[K_MID : K_MID + K_BAND]
            gr[i, b_rows] += g[K_MID + K_BAND :]

    stages = (start, soften, apply, finish, spill)
    held = {b: () for b in range(BLOCKS)}
    for step in range(BLOCKS + len(stages) - 1):
        for i, stage in enumerate(stages):
            if 0 <= step - i < BLOCKS:
                held[step - i] = stage(step - i, *held[step - i])

    joining = spread(1)
    for i in range(2):
        band_left[i] = dot(joining, gl[i].astype(BF16), 1, 0).astype(BF16)
        band_right[i] = dot(joining, gr[i].astype(BF16), 1, 0).astype(BF16)


def put_term(out, term):
    term = term.astype(BF16)
    for yx in range(YH * X):
        for z in range(Z):
            at = (z * YH * X + yx) * 16
            out[yx, z] = term[at : at + 16]


def hidden_kernel(after, h0, h1, h2, h3, hidden, to_above, to_below):
    head = head_index()
    for i, piece in enumerate((h0, h1, h2, h3)):
        hidden[pl.ds(pl.multiple_of((head ^ i) * PIECE, PIECE), PIECE), :] = piece[...]
    to_above[...] = hidden[:EDGE, :]
    to_below[...] = hidden[TOKENS - EDGE :, :]


def first_terms_kernel(grad_q, attn, g0, g1, g2, g3, hidden, out, og, terms, sems):
    head = head_index()
    for i, piece in enumerate((g0, g1, g2, g3)):
        og[pl.ds(pl.multiple_of((head ^ i) * PIECE, PIECE), PIECE), :] = piece[...]
    copies = []
    for i, (left, right) in enumerate(((hidden, grad_q), (og, attn))):
        put_term(terms.at[i], dot(left[...], right[...], 0, 0))
        copies.append(pltpu.make_async_copy(terms.at[i], out.at[:, i], sems.at[i]))
        copies[-1].start()
    for copy in copies:
        copy.wait()


def second_terms_kernel(
    grad_mid, from_left, from_right, hidden, hid_above, hid_below, first,
    out, grads, top, bottom, to_above, to_below,
    hid_mid, terms, sems,
):
    hid_mid[:EDGE] = hid_above[...]
    hid_mid[EDGE : EDGE + TOKENS] = hidden[...]
    hid_mid[EDGE + TOKENS :] = hid_below[...]
    left = pick(0, 0)
    right = pick(TW - DEPTH, 0)
    both = []
    for i in range(2):
        g = grad_mid[i] + dot(left, from_left[i], 1, 0) + dot(right, from_right[i], 1, 0)
        both.append(g.astype(BF16))
        to_above[i] = both[i][:EDGE]
        grads[i] = both[i][EDGE : EDGE + TOKENS]
        top[i] = g[EDGE : 2 * EDGE]
        bottom[i] = g[TOKENS : TOKENS + EDGE]
        to_below[i] = both[i][EDGE + TOKENS :]
    both = jnp.concatenate(both, axis=1)
    copies = []
    width = D // CHUNKS
    deep = Z // CHUNKS
    for c in range(CHUNKS):
        term = dot(hid_mid[:, c * width : (c + 1) * width], both, 0, 0).astype(BF16)
        for i in range(2):
            for yx in range(YH * X):
                for z in range(deep):
                    at = (z * YH * X + yx) * 16
                    here = term[at : at + 16, i * FEAT : (i + 1) * FEAT]
                    terms[i, yx, c * deep + z] = here
        part = pl.ds(c * deep, deep)
        for i in range(2):
            copies.append(
                pltpu.make_async_copy(
                    terms.at[i, :, part], out.at[:, 2 + i, part], sems.at[2 * c + i]
                )
            )
            copies[-1].start()
    for copy in copies:
        copy.wait()


def hidden_grad_kernel(
    grad_q, inner, top, bottom, from_above, from_below, w_qkv_in, keep, send, grads, w_qkv, sem
):
    copy = pltpu.make_async_copy(w_qkv_in, w_qkv, sem)
    copy.start()
    core = lax.axis_index("core")
    for i in range(2):
        grads[i, :EDGE] = (top[i] + from_above[i].astype(F32)).astype(BF16)
        grads[i, EDGE : TOKENS - EDGE] = inner[i, EDGE : TOKENS - EDGE]
        grads[i, TOKENS - EDGE :] = (bottom[i] + from_below[i].astype(F32)).astype(BF16)
    copy.wait()
    for yl in range(YL):
        for out, c in ((send, 1 - core), (keep, core)):
            at = pl.ds(pl.multiple_of((yl * CORE + c) * PIECE, PIECE), PIECE)
            total = dot(grad_q[at, :], w_qkv[0], 1, 1)
            for j in range(2):
                total += dot(grads[j, at, :], w_qkv[1 + j], 1, 1)
            out[yl] = total.astype(BF16)


def halve_kernel(keep, got, stay, send):
    yl = lax.axis_index("yl")
    stay[...] = keep[yl].astype(F32) + got[yl].astype(F32)
    send[...] = (keep[1 - yl].astype(F32) + got[1 - yl].astype(F32)).astype(BF16)


def summed(terms):
    total = terms[0].astype(F32)
    for i in range(1, 8):
        total += terms[i].astype(F32)
    return total


def sum_kernel(terms, out):
    for j in range(4):
        total = terms[0, j].astype(F32)
        for i in range(1, YH * X):
            total += terms[i, j].astype(F32)
        out[:, :, j * FEAT : (j + 1) * FEAT] = total.astype(BF16)


def last_kernel(parts, grad_wqkv, grad_wout):
    total = summed(parts)
    grad_wqkv[0] = total[:, :FEAT]
    grad_wout[...] = total[:, FEAT : 2 * FEAT]
    grad_wqkv[1] = total[:, 2 * FEAT : 3 * FEAT]
    grad_wqkv[2] = total[:, 3 * FEAT :]


def ring(size, step):
    return [(i, (i + step) % size) for i in range(size)]


SWAP = [(0, 1), (1, 0)]
COLS = ("yh", "x", "yl")


def columns(step):
    pairs = []
    for col in range(YH * X):
        for yl in range(YL):
            to = col + step
            to_yl = yl if 0 <= to < YH * X else 1 - yl
            pairs.append((col * YL + yl, (to % (YH * X)) * YL + to_yl))
    return pairs


def per_device(hidden_in, queries, keys, values, w_qkv, w_out, out_grad):
    q = queries.reshape(TOKENS, FEAT)
    k = keys.reshape(TOKENS, FEAT)
    v = values.reshape(TOKENS, FEAT)
    w3 = w_qkv.transpose(1, 0, 2)

    flat = shaped((TOKENS, FEAT))
    edge = shaped((2, EDGE, FEAT))
    band = shaped((2, SENT, FEAT))
    mids = shaped((2, CENTER, FEAT))
    own = shaped((PIECE, D))
    own_grad = out_grad.reshape(PIECE, D)
    own_hidden = hidden_in.reshape(PIECE, D)
    to_above, to_below = call(
        edges_kernel, (edge, edge), scratch=[pltpu.SemaphoreType.DMA((4,))], n_in=2, hbm=(0, 1)
    )(k, v)
    below = lax.ppermute(to_above, "z", ring(Z, -1))
    above = lax.ppermute(to_below, "z", ring(Z, 1))
    q, kv, w_out, g0, h0 = call(
        load_kernel,
        (flat, shaped((2, TOKENS, FEAT)), shaped((FEAT, D)), own, own),
        scratch=[pltpu.SemaphoreType.DMA((6,))],
        n_in=7,
        hbm=range(1, 7),
        flops=10_000_000_000,
    )(to_above, q, k, v, w_out, own_grad, own_hidden)
    g2 = lax.ppermute(own_grad, "yl", SWAP)
    late, _ = lax.optimization_barrier((own_hidden, below))
    h2 = lax.ppermute(late, "yl", SWAP)

    mid, to_left, to_right = call(bands_kernel, (mids, band, band), n_in=3)(kv, above, below)
    from_right = lax.ppermute(to_left, COLS, columns(-1))
    from_left = lax.ppermute(to_right, COLS, columns(1))
    g2, _ = lax.optimization_barrier((g2, to_left))
    g3 = lax.ppermute(g2, "core", SWAP)
    g1 = lax.ppermute(g0, "core", SWAP)
    h1 = lax.ppermute(h0, "core", SWAP)
    h2, _, _ = lax.optimization_barrier((h2, from_left, from_right))
    h3 = lax.ppermute(h2, "core", SWAP)

    attn, grad_q, grad_mid, band_left, band_right = call(
        attention_kernel,
        (flat, flat, shaped((2, CENTER, FEAT), F32), band, band),
        scratch=[
            pltpu.VMEM((TOKENS, FEAT), BF16),
            pltpu.VMEM((2, BAND, FEAT), F32),
            pltpu.VMEM((2, BAND, FEAT), F32),
            pltpu.VMEM((2, BAND, FEAT), BF16),
            pltpu.VMEM((2, BAND, FEAT), BF16),
        ],
        n_in=9,
    )(q, g0, g1, g2, g3, w_out, mid, from_left, from_right)

    got_right = lax.ppermute(band_left, COLS, columns(-1))
    got_left = lax.ppermute(band_right, COLS, columns(1))
    hid_edge = shaped((EDGE, D))
    hidden, to_above, to_below = call(
        hidden_kernel, (shaped((TOKENS, D)), hid_edge, hid_edge), n_in=5
    )(band_left, h0, h1, h2, h3)
    hid_below = lax.ppermute(to_above, "z", ring(Z, -1))
    hid_above = lax.ppermute(to_below, "z", ring(Z, 1))
    all_terms = shaped((YH * X, 4, Z, 16, FEAT))
    (terms,) = call(
        first_terms_kernel,
        (all_terms,),
        scratch=[
            pltpu.VMEM((TOKENS, D), BF16),
            pltpu.VMEM((2, YH * X, Z, 16, FEAT), BF16),
            pltpu.SemaphoreType.DMA((2,)),
        ],
        n_in=7,
        hbm_out=(0,),
        flops=10_000_000_000,
    )(grad_q, attn, g0, g1, g2, g3, hidden)
    edge32 = shaped((2, EDGE, FEAT), F32)
    terms, grads, top, bottom, to_above, to_below = call(
        second_terms_kernel,
        (all_terms, shaped((2, TOKENS, FEAT)), edge32, edge32, edge, edge),
        scratch=[
            pltpu.VMEM((CENTER, D), BF16),
            pltpu.VMEM((2, YH * X, Z, 16, FEAT), BF16),
            pltpu.SemaphoreType.DMA((2 * CHUNKS,)),
        ],
        n_in=7,
        hbm=(6,),
        hbm_out=(0,),
        alias={6: 0},
    )(grad_mid, got_left, got_right, hidden, hid_above, hid_below, terms)
    got_below = lax.ppermute(to_above, "z", ring(Z, -1))
    got_above = lax.ppermute(to_below, "z", ring(Z, 1))
    terms = lax.all_to_all(terms, YX, 0, 0, tiled=True)

    half = shaped((YL, PIECE, D))
    keep, send = call(
        hidden_grad_kernel,
        (half, half),
        scratch=[
            pltpu.VMEM((2, TOKENS, FEAT), BF16),
            pltpu.VMEM((3, D, FEAT), BF16),
            pltpu.SemaphoreType.DMA,
        ],
        n_in=7,
        hbm=(6,),
    )(grad_q, grads, top, bottom, got_above, got_below, w3)
    got = lax.ppermute(send, "core", SWAP)
    stay, send = call(halve_kernel, (shaped((PIECE, D), F32), shaped((PIECE, D))), n_in=2)(keep, got)
    got = lax.ppermute(send, "yl", SWAP)
    grad_hidden = (stay + got.astype(F32)).astype(BF16).reshape(1, 8, TW, D)

    (parts,) = call(sum_kernel, (shaped((Z, 16, 4 * FEAT)),), n_in=1)(terms)
    parts = lax.all_to_all(parts, "z", 0, 0, tiled=True)
    grad_wqkv, grad_wout = call(
        last_kernel, (shaped((3, 16, FEAT), F32), shaped((16, FEAT), F32)), n_in=1
    )(parts)
    return grad_hidden, grad_wqkv.transpose(1, 0, 2), grad_wout.T


def solution(mesh):
    fine = Mesh(mesh.devices.reshape(Z, YH, X, YL, CORE), GRID + HEAD)
    return jax.shard_map(
        per_device,
        mesh=fine,
        in_specs=(
            P(GRID, HEAD, None, None),
            P(GRID, None, None, HEAD),
            P(GRID, None, None, HEAD),
            P(GRID, None, None, HEAD),
            P(None, None, HEAD),
            P(HEAD, None),
            P(GRID, HEAD, None, None),
        ),
        out_specs=(P(GRID, HEAD, None, None), P(GRID, None, HEAD), P(HEAD, GRID)),
        check_vma=False,
    )
```

```python
import jax
import jax.numpy as jnp
from jax import lax
from jax.experimental import pallas as pl
from jax.experimental.pallas import tpu as pltpu
from jax.sharding import Mesh
from jax.sharding import PartitionSpec as P

D = 1024
HD = 64
HEADS_HERE = 4
FEAT = HD * HEADS_HERE
TH = 32
TW = 16
TOKENS = TH * TW
DEPTH = 3
IMG_H = 256
IMG_W = 128
PAD_H = TH + 2 * DEPTH
CENTER = PAD_H * TW
EDGE = DEPTH * TW
SLOTS = 4
BAND = 40 * SLOTS
SENT = 128
CHUNKS = 4
PIECE = TOKENS // 4
BLOCKS = 8
BLK = TOKENS // BLOCKS
BLK_ROWS = TH // BLOCKS
K_MID = (BLK_ROWS + 2 * DEPTH) * TW
K_BAND = 12 * SLOTS
K_ALL = K_MID + 2 * K_BAND
Z, YH, X, YL, CORE = 8, 2, 4, 2, 2
GRID = ("z", "yh", "xh", "xl")
HEAD = ("yl", "core")
F32 = jnp.float32
BF16 = jnp.bfloat16
VMEM_LIMIT = 24 * 1024 * 1024


def dot(a, b, ca, cb):
    return lax.dot_general(a, b, (((ca,), (cb,)), ((), ())), preferred_element_type=F32)


def call(body, out_shape, scratch=(), n_in=0, hbm=(), hbm_out=(), flops=0, alias=None):
    specs = [pl.BlockSpec(memory_space=pltpu.HBM if i in hbm else pltpu.VMEM) for i in range(n_in)]
    outs = [
        pl.BlockSpec(memory_space=pltpu.HBM if i in hbm_out else pltpu.VMEM)
        for i in range(len(out_shape))
    ]
    out_shape = [
        pltpu.HBM(o.shape, o.dtype) if i in hbm_out else o for i, o in enumerate(out_shape)
    ]
    run = pl.pallas_call(
        body,
        out_shape=out_shape,
        in_specs=specs,
        out_specs=outs,
        scratch_shapes=list(scratch),
        input_output_aliases=alias or {},
        compiler_params=pltpu.CompilerParams(vmem_limit_bytes=VMEM_LIMIT),
        cost_estimate=pl.CostEstimate(flops=flops, bytes_accessed=0, transcendentals=0),
    )

    def on(*args):
        hold = pltpu.with_memory_space_constraint
        return run(*(hold(a, pltpu.HBM) if i in hbm else a for i, a in enumerate(args)))

    return on


def head_index():
    return lax.axis_index("yl") * CORE + lax.axis_index("core")


def shaped(shape, dtype=BF16):
    return jax.ShapeDtypeStruct(shape, dtype)


def pick(first_col, token_axis):
    shape = (CENTER, SENT) if token_axis == 0 else (SENT, CENTER)
    token = lax.broadcasted_iota(jnp.int32, shape, token_axis)
    sent = lax.broadcasted_iota(jnp.int32, shape, 1 - token_axis)
    row = (sent * 171) >> 9
    wanted = row * TW + first_col + sent - DEPTH * row
    return jnp.where((token == wanted) & (row < PAD_H), 1.0, 0.0).astype(BF16)


def spread(band_axis):
    shape = (BAND, SENT) if band_axis == 0 else (SENT, BAND)
    slot = lax.broadcasted_iota(jnp.int32, shape, band_axis)
    sent = lax.broadcasted_iota(jnp.int32, shape, 1 - band_axis)
    lane = slot & (SLOTS - 1)
    wanted = (slot // SLOTS) * DEPTH + lane
    return jnp.where((sent == wanted) & (lane < DEPTH) & (slot < PAD_H * SLOTS), 1.0, 0.0).astype(BF16)


def copy_all(pairs, sems):
    copies = [pltpu.make_async_copy(a, b, sems.at[i]) for i, (a, b) in enumerate(pairs)]
    for copy in copies:
        copy.start()
    for copy in copies:
        copy.wait()


def edges_kernel(k, v, to_above, to_below, sems):
    first, last = pl.ds(0, EDGE), pl.ds(TOKENS - EDGE, EDGE)
    pairs = [(k.at[first], to_above.at[0]), (v.at[first], to_above.at[1])]
    pairs += [(k.at[last], to_below.at[0]), (v.at[last], to_below.at[1])]
    copy_all(pairs, sems)


def load_kernel(
    after, q, k, v, w_out, out_grad, hidden, q_out, kv, w_out_out, own_grad, own_hidden, sems
):
    pairs = [(out_grad, own_grad), (hidden, own_hidden), (k, kv.at[0]), (v, kv.at[1])]
    copy_all(pairs + [(q, q_out), (w_out, w_out_out)], sems)


def bands_kernel(kv, above, below, mid, to_left, to_right):
    left = pick(0, 1)
    right = pick(TW - DEPTH, 1)
    for i in range(2):
        mid[i, :EDGE] = above[i]
        mid[i, EDGE : EDGE + TOKENS] = kv[i]
        mid[i, EDGE + TOKENS :] = below[i]
        to_left[i] = dot(left, mid[i], 1, 0).astype(BF16)
        to_right[i] = dot(right, mid[i], 1, 0).astype(BF16)


def stacked(x):
    lane = lax.broadcasted_iota(jnp.int32, x.shape, 1) // HD
    zero = jnp.zeros_like(x)
    return jnp.concatenate([jnp.where(lane == h, x, zero) for h in range(HEADS_HERE)], axis=0)


def unstacked(x):
    lane = lax.broadcasted_iota(jnp.int32, (BLK, FEAT), 1) // HD
    out = x[:BLK]
    for h in range(1, HEADS_HERE):
        out = jnp.where(lane == h, x[h * BLK : (h + 1) * BLK], out)
    return out


def block_of(b):
    rows = slice(b * BLK, (b + 1) * BLK)
    m_rows = slice(b * BLK, b * BLK + K_MID)
    b_rows = slice(b * BLK_ROWS * SLOTS, b * BLK_ROWS * SLOTS + K_BAND)
    return rows, m_rows, b_rows


def attention_kernel(
    q, og0, og1, og2, og3, w_out, mid, sent_left, sent_right,
    attn_out, grad_q, grad_mid, band_left, band_right,
    ga, gl, gr, from_left, from_right,
):
    head = head_index()
    tile_row = lax.axis_index("z")
    tile_col = lax.axis_index("yh") * X + lax.axis_index("xh") * 2 + lax.axis_index("xl")
    for i, piece in enumerate((og0, og1, og2, og3)):
        at = pl.multiple_of((head ^ i) * PIECE, PIECE)
        ga[pl.ds(at, PIECE), :] = dot(piece[...], w_out[...], 1, 1).astype(BF16)
    spreading = spread(0)
    for i in range(2):
        from_left[i] = dot(spreading, sent_left[i], 1, 0).astype(BF16)
        from_right[i] = dot(spreading, sent_right[i], 1, 0).astype(BF16)
    grad_mid[...] = jnp.zeros_like(grad_mid)
    gl[...] = jnp.zeros_like(gl)
    gr[...] = jnp.zeros_like(gr)

    key = lax.broadcasted_iota(jnp.int32, (1, K_ALL), 1)
    in_mid = key < K_MID
    in_left = key < K_MID + K_BAND
    slot = key & (SLOTS - 1)
    key_row = jnp.where(
        in_mid,
        key // TW,
        jnp.where(in_left, (key - K_MID) // SLOTS, (key - K_MID - K_BAND) // SLOTS),
    )
    band_col = jnp.where(in_left, slot, TW + DEPTH + slot)
    key_col = jnp.where(in_mid, (key & (TW - 1)) + DEPTH, jnp.where(slot < DEPTH, band_col, 1000))
    col_image = tile_col * TW + key_col - DEPTH
    key_col = jnp.where((col_image >= 0) & (col_image < IMG_W), key_col, 1000)
    token = lax.broadcasted_iota(jnp.int32, (BLK, 1), 0)
    row_off = key_row - token // TW
    col_off = key_col - (token & (TW - 1))
    near = (row_off >= 0) & (row_off < 7) & (col_off >= 0) & (col_off < 7)
    row_image = tile_row * TH + key_row - DEPTH

    def start(b):
        rows, m_rows, b_rows = block_of(b)
        kk = jnp.concatenate([mid[0, m_rows], from_left[0, b_rows], from_right[0, b_rows]], axis=0)
        vv = jnp.concatenate([mid[1, m_rows], from_left[1, b_rows], from_right[1, b_rows]], axis=0)
        qs = stacked(q[rows, :] * jnp.asarray(HD**-0.5, BF16))
        gs = stacked(ga[rows, :])
        return kk, vv, qs, gs, dot(qs, kk, 1, 1), dot(gs, vv, 1, 1)

    def soften(b, kk, vv, qs, gs, s, dprob):
        row_here = row_image + b * BLK_ROWS
        valid = near & (row_here >= 0) & (row_here < IMG_H)
        bias = jnp.where(valid, 0.0, -jnp.inf).astype(F32)
        s = (s.reshape(HEADS_HERE, BLK, K_ALL) + bias[None]).reshape(HEADS_HERE * BLK, K_ALL)
        e = jnp.exp(s - jnp.max(s, axis=1, keepdims=True))
        p = e * (1.0 / jnp.sum(e, axis=1, keepdims=True))
        return kk, vv, qs, gs, dprob, p, p.astype(BF16)

    def apply(b, kk, vv, qs, gs, dprob, p, p16):
        return kk, qs, gs, dprob, p, dot(p16, vv, 1, 0).astype(BF16), dot(p16, gs, 0, 0)

    def finish(b, kk, qs, gs, dprob, p, attn, grad_v):
        rows, m_rows, b_rows = block_of(b)
        attn_out[rows, :] = unstacked(attn)
        delta = jnp.sum(gs.astype(F32) * attn.astype(F32), axis=1, keepdims=True)
        return kk, qs, (p * (dprob - delta)).astype(BF16), grad_v

    def spill(b, kk, qs, ds, grad_v):
        rows, m_rows, b_rows = block_of(b)
        grad_q[rows, :] = unstacked(dot(ds, kk, 1, 0) * (HD**-0.5)).astype(BF16)
        for i, g in enumerate((dot(ds, qs, 0, 0), grad_v)):
            grad_mid[i, m_rows] += g[:K_MID]
            gl[i, b_rows] += g[K_MID : K_MID + K_BAND]
            gr[i, b_rows] += g[K_MID + K_BAND :]

    stages = (start, soften, apply, finish, spill)
    held = {b: () for b in range(BLOCKS)}
    for step in range(BLOCKS + len(stages) - 1):
        for i, stage in enumerate(stages):
            if 0 <= step - i < BLOCKS:
                held[step - i] = stage(step - i, *held[step - i])

    joining = spread(1)
    for i in range(2):
        band_left[i] = dot(joining, gl[i].astype(BF16), 1, 0).astype(BF16)
        band_right[i] = dot(joining, gr[i].astype(BF16), 1, 0).astype(BF16)


def slot(yx):
    return (yx // X) * X + (yx % 2) * 2 + (yx % X) // 2


def put_term(out, term):
    term = term.astype(BF16)
    for yx in range(YH * X):
        for z in range(Z):
            at = (z * YH * X + yx) * 16
            out[slot(yx), z] = term[at : at + 16]


def hidden_kernel(after, h0, h1, h2, h3, hidden, to_above, to_below):
    head = head_index()
    for i, piece in enumerate((h0, h1, h2, h3)):
        hidden[pl.ds(pl.multiple_of((head ^ i) * PIECE, PIECE), PIECE), :] = piece[...]
    to_above[...] = hidden[:EDGE, :]
    to_below[...] = hidden[TOKENS - EDGE :, :]


def first_terms_kernel(grad_q, attn, g0, g1, g2, g3, hidden, out, og, terms, sems):
    head = head_index()
    for i, piece in enumerate((g0, g1, g2, g3)):
        og[pl.ds(pl.multiple_of((head ^ i) * PIECE, PIECE), PIECE), :] = piece[...]
    copies = []
    for i, (left, right) in enumerate(((hidden, grad_q), (og, attn))):
        put_term(terms.at[i], dot(left[...], right[...], 0, 0))
        copies.append(pltpu.make_async_copy(terms.at[i], out.at[:, i], sems.at[i]))
        copies[-1].start()
    for copy in copies:
        copy.wait()


def second_terms_kernel(
    grad_mid, from_left, from_right, hidden, hid_above, hid_below, first,
    out, grads, top, bottom, to_above, to_below,
    hid_mid, terms, sems,
):
    hid_mid[:EDGE] = hid_above[...]
    hid_mid[EDGE : EDGE + TOKENS] = hidden[...]
    hid_mid[EDGE + TOKENS :] = hid_below[...]
    left = pick(0, 0)
    right = pick(TW - DEPTH, 0)
    both = []
    for i in range(2):
        g = grad_mid[i] + dot(left, from_left[i], 1, 0) + dot(right, from_right[i], 1, 0)
        both.append(g.astype(BF16))
        to_above[i] = both[i][:EDGE]
        grads[i] = both[i][EDGE : EDGE + TOKENS]
        top[i] = g[EDGE : 2 * EDGE]
        bottom[i] = g[TOKENS : TOKENS + EDGE]
        to_below[i] = both[i][EDGE + TOKENS :]
    both = jnp.concatenate(both, axis=1)
    copies = []
    width = D // CHUNKS
    deep = Z // CHUNKS
    for c in range(CHUNKS):
        term = dot(hid_mid[:, c * width : (c + 1) * width], both, 0, 0).astype(BF16)
        for i in range(2):
            for yx in range(YH * X):
                for z in range(deep):
                    at = (z * YH * X + yx) * 16
                    here = term[at : at + 16, i * FEAT : (i + 1) * FEAT]
                    terms[i, slot(yx), c * deep + z] = here
        part = pl.ds(c * deep, deep)
        for i in range(2):
            copies.append(
                pltpu.make_async_copy(
                    terms.at[i, :, part], out.at[:, 2 + i, part], sems.at[2 * c + i]
                )
            )
            copies[-1].start()
    for copy in copies:
        copy.wait()


def hidden_grad_kernel(
    grad_q, inner, top, bottom, from_above, from_below, w_qkv_in, keep, send, grads, w_qkv, sem
):
    copy = pltpu.make_async_copy(w_qkv_in, w_qkv, sem)
    copy.start()
    core = lax.axis_index("core")
    for i in range(2):
        grads[i, :EDGE] = (top[i] + from_above[i].astype(F32)).astype(BF16)
        grads[i, EDGE : TOKENS - EDGE] = inner[i, EDGE : TOKENS - EDGE]
        grads[i, TOKENS - EDGE :] = (bottom[i] + from_below[i].astype(F32)).astype(BF16)
    copy.wait()
    for yl in range(YL):
        for out, c in ((send, 1 - core), (keep, core)):
            at = pl.ds(pl.multiple_of((yl * CORE + c) * PIECE, PIECE), PIECE)
            total = dot(grad_q[at, :], w_qkv[0], 1, 1)
            for j in range(2):
                total += dot(grads[j, at, :], w_qkv[1 + j], 1, 1)
            out[yl] = total.astype(BF16)


def halve_kernel(keep, got, stay, send):
    yl = lax.axis_index("yl")
    stay[...] = keep[yl].astype(F32) + got[yl].astype(F32)
    send[...] = (keep[1 - yl].astype(F32) + got[1 - yl].astype(F32)).astype(BF16)


def summed(terms):
    total = terms[0].astype(F32)
    for i in range(1, 8):
        total += terms[i].astype(F32)
    return total


def sum_kernel(terms, out):
    for j in range(4):
        total = terms[0, j].astype(F32)
        for i in range(1, YH * X):
            total += terms[i, j].astype(F32)
        out[:, :, j * FEAT : (j + 1) * FEAT] = total.astype(BF16)


def last_kernel(parts, grad_wqkv, grad_wout):
    total = summed(parts)
    grad_wqkv[0] = total[:, :FEAT]
    grad_wout[...] = total[:, FEAT : 2 * FEAT]
    grad_wqkv[1] = total[:, 2 * FEAT : 3 * FEAT]
    grad_wqkv[2] = total[:, 3 * FEAT :]


def ring(size, step):
    return [(i, (i + step) % size) for i in range(size)]


SWAP = [(0, 1), (1, 0)]
COLS = ("yh", "xh", "xl", "yl")


def columns(step):
    pairs = []
    for col in range(YH * X):
        for yl in range(YL):
            to = col + step
            to_yl = yl if 0 <= to < YH * X else 1 - yl
            pairs.append((col * YL + yl, (to % (YH * X)) * YL + to_yl))
    return pairs


def per_device(hidden_in, queries, keys, values, w_qkv, w_out, out_grad):
    q = queries.reshape(TOKENS, FEAT)
    k = keys.reshape(TOKENS, FEAT)
    v = values.reshape(TOKENS, FEAT)
    w3 = w_qkv.transpose(1, 0, 2)

    flat = shaped((TOKENS, FEAT))
    edge = shaped((2, EDGE, FEAT))
    band = shaped((2, SENT, FEAT))
    mids = shaped((2, CENTER, FEAT))
    own = shaped((PIECE, D))
    own_grad = out_grad.reshape(PIECE, D)
    own_hidden = hidden_in.reshape(PIECE, D)
    to_above, to_below = call(
        edges_kernel, (edge, edge), scratch=[pltpu.SemaphoreType.DMA((4,))], n_in=2, hbm=(0, 1)
    )(k, v)
    below = lax.ppermute(to_above, "z", ring(Z, -1))
    above = lax.ppermute(to_below, "z", ring(Z, 1))
    q, kv, w_out, g0, h0 = call(
        load_kernel,
        (flat, shaped((2, TOKENS, FEAT)), shaped((FEAT, D)), own, own),
        scratch=[pltpu.SemaphoreType.DMA((6,))],
        n_in=7,
        hbm=range(1, 7),
        flops=10_000_000_000,
    )(to_above, q, k, v, w_out, own_grad, own_hidden)
    g2 = lax.ppermute(own_grad, "yl", SWAP)
    late, _ = lax.optimization_barrier((own_hidden, below))
    h2 = lax.ppermute(late, "yl", SWAP)

    mid, to_left, to_right = call(bands_kernel, (mids, band, band), n_in=3)(kv, above, below)
    from_right = lax.ppermute(to_left, COLS, columns(-1))
    from_left = lax.ppermute(to_right, COLS, columns(1))
    g2, _ = lax.optimization_barrier((g2, to_left))
    g3 = lax.ppermute(g2, "core", SWAP)
    g1 = lax.ppermute(g0, "core", SWAP)
    h1 = lax.ppermute(h0, "core", SWAP)
    h2, _, _ = lax.optimization_barrier((h2, from_left, from_right))
    h3 = lax.ppermute(h2, "core", SWAP)

    attn, grad_q, grad_mid, band_left, band_right = call(
        attention_kernel,
        (flat, flat, shaped((2, CENTER, FEAT), F32), band, band),
        scratch=[
            pltpu.VMEM((TOKENS, FEAT), BF16),
            pltpu.VMEM((2, BAND, FEAT), F32),
            pltpu.VMEM((2, BAND, FEAT), F32),
            pltpu.VMEM((2, BAND, FEAT), BF16),
            pltpu.VMEM((2, BAND, FEAT), BF16),
        ],
        n_in=9,
    )(q, g0, g1, g2, g3, w_out, mid, from_left, from_right)

    got_right = lax.ppermute(band_left, COLS, columns(-1))
    got_left = lax.ppermute(band_right, COLS, columns(1))
    hid_edge = shaped((EDGE, D))
    hidden, to_above, to_below = call(
        hidden_kernel, (shaped((TOKENS, D)), hid_edge, hid_edge), n_in=5
    )(band_left, h0, h1, h2, h3)
    hid_below = lax.ppermute(to_above, "z", ring(Z, -1))
    hid_above = lax.ppermute(to_below, "z", ring(Z, 1))
    all_terms = shaped((YH * X, 4, Z, 16, FEAT))
    (terms,) = call(
        first_terms_kernel,
        (all_terms,),
        scratch=[
            pltpu.VMEM((TOKENS, D), BF16),
            pltpu.VMEM((2, YH * X, Z, 16, FEAT), BF16),
            pltpu.SemaphoreType.DMA((2,)),
        ],
        n_in=7,
        hbm_out=(0,),
        flops=10_000_000_000,
    )(grad_q, attn, g0, g1, g2, g3, hidden)
    edge32 = shaped((2, EDGE, FEAT), F32)
    terms, grads, top, bottom, to_above, to_below = call(
        second_terms_kernel,
        (all_terms, shaped((2, TOKENS, FEAT)), edge32, edge32, edge, edge),
        scratch=[
            pltpu.VMEM((CENTER, D), BF16),
            pltpu.VMEM((2, YH * X, Z, 16, FEAT), BF16),
            pltpu.SemaphoreType.DMA((2 * CHUNKS,)),
        ],
        n_in=7,
        hbm=(6,),
        hbm_out=(0,),
        alias={6: 0},
    )(grad_mid, got_left, got_right, hidden, hid_above, hid_below, terms)
    got_below = lax.ppermute(to_above, "z", ring(Z, -1))
    got_above = lax.ppermute(to_below, "z", ring(Z, 1))
    terms = lax.all_to_all(terms, ("yh", "xl", "xh"), 0, 0, tiled=True)

    half = shaped((YL, PIECE, D))
    keep, send = call(
        hidden_grad_kernel,
        (half, half),
        scratch=[
            pltpu.VMEM((2, TOKENS, FEAT), BF16),
            pltpu.VMEM((3, D, FEAT), BF16),
            pltpu.SemaphoreType.DMA,
        ],
        n_in=7,
        hbm=(6,),
    )(grad_q, grads, top, bottom, got_above, got_below, w3)
    got = lax.ppermute(send, "core", SWAP)
    stay, send = call(halve_kernel, (shaped((PIECE, D), F32), shaped((PIECE, D))), n_in=2)(keep, got)
    got = lax.ppermute(send, "yl", SWAP)
    grad_hidden = (stay + got.astype(F32)).astype(BF16).reshape(1, 8, TW, D)

    (parts,) = call(sum_kernel, (shaped((Z, 16, 4 * FEAT)),), n_in=1)(terms)
    parts = lax.all_to_all(parts, "z", 0, 0, tiled=True)
    grad_wqkv, grad_wout = call(
        last_kernel, (shaped((3, 16, FEAT), F32), shaped((16, FEAT), F32)), n_in=1
    )(parts)
    return grad_hidden, grad_wqkv.transpose(1, 0, 2), grad_wout.T


def solution(mesh):
    fine = Mesh(mesh.devices.reshape(Z, YH, 2, 2, YL, CORE), GRID + HEAD)
    return jax.shard_map(
        per_device,
        mesh=fine,
        in_specs=(
            P(GRID, HEAD, None, None),
            P(GRID, None, None, HEAD),
            P(GRID, None, None, HEAD),
            P(GRID, None, None, HEAD),
            P(None, None, HEAD),
            P(HEAD, None),
            P(GRID, HEAD, None, None),
        ),
        out_specs=(P(GRID, HEAD, None, None), P(GRID, None, HEAD), P(HEAD, GRID)),
        check_vma=False,
    )
```

```python
import jax
import jax.numpy as jnp
from jax import lax
from jax.experimental import pallas as pl
from jax.experimental.pallas import tpu as pltpu
from jax.sharding import Mesh
from jax.sharding import PartitionSpec as P

D = 1024
HD = 64
HEADS_HERE = 4
FEAT = HD * HEADS_HERE
TH = 32
TW = 16
TOKENS = TH * TW
DEPTH = 3
IMG_H = 256
IMG_W = 128
PAD_H = TH + 2 * DEPTH
CENTER = PAD_H * TW
EDGE = DEPTH * TW
SLOTS = 4
BAND = 40 * SLOTS
SENT = 128
CHUNKS = 4
PIECE = TOKENS // 4
BLOCKS = 8
BLK = TOKENS // BLOCKS
BLK_ROWS = TH // BLOCKS
K_MID = (BLK_ROWS + 2 * DEPTH) * TW
K_BAND = 12 * SLOTS
K_ALL = K_MID + 2 * K_BAND
Z, YH, X, YL, CORE = 8, 2, 4, 2, 2
ZZ = ("zh", "zl")
GRID = ZZ + ("yh", "xh", "xl")
HEAD = ("yl", "core")
F32 = jnp.float32
BF16 = jnp.bfloat16
VMEM_LIMIT = 24 * 1024 * 1024


def dot(a, b, ca, cb):
    return lax.dot_general(a, b, (((ca,), (cb,)), ((), ())), preferred_element_type=F32)


def call(body, out_shape, scratch=(), n_in=0, hbm=(), hbm_out=(), flops=0, alias=None):
    specs = [pl.BlockSpec(memory_space=pltpu.HBM if i in hbm else pltpu.VMEM) for i in range(n_in)]
    outs = [
        pl.BlockSpec(memory_space=pltpu.HBM if i in hbm_out else pltpu.VMEM)
        for i in range(len(out_shape))
    ]
    out_shape = [
        pltpu.HBM(o.shape, o.dtype) if i in hbm_out else o for i, o in enumerate(out_shape)
    ]
    run = pl.pallas_call(
        body,
        out_shape=out_shape,
        in_specs=specs,
        out_specs=outs,
        scratch_shapes=list(scratch),
        input_output_aliases=alias or {},
        compiler_params=pltpu.CompilerParams(vmem_limit_bytes=VMEM_LIMIT),
        cost_estimate=pl.CostEstimate(flops=flops, bytes_accessed=0, transcendentals=0),
    )

    def on(*args):
        hold = pltpu.with_memory_space_constraint
        return run(*(hold(a, pltpu.HBM) if i in hbm else a for i, a in enumerate(args)))

    return on


def head_index():
    return lax.axis_index("yl") * CORE + lax.axis_index("core")


def shaped(shape, dtype=BF16):
    return jax.ShapeDtypeStruct(shape, dtype)


def pick(first_col, token_axis):
    shape = (CENTER, SENT) if token_axis == 0 else (SENT, CENTER)
    token = lax.broadcasted_iota(jnp.int32, shape, token_axis)
    sent = lax.broadcasted_iota(jnp.int32, shape, 1 - token_axis)
    row = (sent * 171) >> 9
    wanted = row * TW + first_col + sent - DEPTH * row
    return jnp.where((token == wanted) & (row < PAD_H), 1.0, 0.0).astype(BF16)


def spread(band_axis):
    shape = (BAND, SENT) if band_axis == 0 else (SENT, BAND)
    slot = lax.broadcasted_iota(jnp.int32, shape, band_axis)
    sent = lax.broadcasted_iota(jnp.int32, shape, 1 - band_axis)
    lane = slot & (SLOTS - 1)
    wanted = (slot // SLOTS) * DEPTH + lane
    return jnp.where((sent == wanted) & (lane < DEPTH) & (slot < PAD_H * SLOTS), 1.0, 0.0).astype(BF16)


def copy_all(pairs, sems):
    copies = [pltpu.make_async_copy(a, b, sems.at[i]) for i, (a, b) in enumerate(pairs)]
    for copy in copies:
        copy.start()
    for copy in copies:
        copy.wait()


def edges_kernel(k, v, to_above, to_below, sems):
    first, last = pl.ds(0, EDGE), pl.ds(TOKENS - EDGE, EDGE)
    pairs = [(k.at[first], to_above.at[0]), (v.at[first], to_above.at[1])]
    pairs += [(k.at[last], to_below.at[0]), (v.at[last], to_below.at[1])]
    copy_all(pairs, sems)


def load_kernel(
    after, q, k, v, w_out, out_grad, hidden, q_out, kv, w_out_out, own_grad, own_hidden, sems
):
    pairs = [(out_grad, own_grad), (hidden, own_hidden), (k, kv.at[0]), (v, kv.at[1])]
    copy_all(pairs + [(q, q_out), (w_out, w_out_out)], sems)


def bands_kernel(kv, above, below, mid, to_left, to_right):
    left = pick(0, 1)
    right = pick(TW - DEPTH, 1)
    for i in range(2):
        mid[i, :EDGE] = above[i]
        mid[i, EDGE : EDGE + TOKENS] = kv[i]
        mid[i, EDGE + TOKENS :] = below[i]
        to_left[i] = dot(left, mid[i], 1, 0).astype(BF16)
        to_right[i] = dot(right, mid[i], 1, 0).astype(BF16)


def stacked(x):
    lane = lax.broadcasted_iota(jnp.int32, x.shape, 1) // HD
    zero = jnp.zeros_like(x)
    return jnp.concatenate([jnp.where(lane == h, x, zero) for h in range(HEADS_HERE)], axis=0)


def unstacked(x):
    lane = lax.broadcasted_iota(jnp.int32, (BLK, FEAT), 1) // HD
    out = x[:BLK]
    for h in range(1, HEADS_HERE):
        out = jnp.where(lane == h, x[h * BLK : (h + 1) * BLK], out)
    return out


def block_of(b):
    rows = slice(b * BLK, (b + 1) * BLK)
    m_rows = slice(b * BLK, b * BLK + K_MID)
    b_rows = slice(b * BLK_ROWS * SLOTS, b * BLK_ROWS * SLOTS + K_BAND)
    return rows, m_rows, b_rows


def attention_kernel(
    q, og0, og1, og2, og3, w_out, mid, sent_left, sent_right,
    attn_out, grad_q, grad_mid, band_left, band_right,
    ga, gl, gr, from_left, from_right,
):
    head = head_index()
    tile_row = lax.axis_index("zh") * 2 + lax.axis_index("zl")
    tile_col = lax.axis_index("yh") * X + lax.axis_index("xh") * 2 + lax.axis_index("xl")
    for i, piece in enumerate((og0, og1, og2, og3)):
        at = pl.multiple_of((head ^ i) * PIECE, PIECE)
        ga[pl.ds(at, PIECE), :] = dot(piece[...], w_out[...], 1, 1).astype(BF16)
    spreading = spread(0)
    for i in range(2):
        from_left[i] = dot(spreading, sent_left[i], 1, 0).astype(BF16)
        from_right[i] = dot(spreading, sent_right[i], 1, 0).astype(BF16)
    grad_mid[...] = jnp.zeros_like(grad_mid)
    gl[...] = jnp.zeros_like(gl)
    gr[...] = jnp.zeros_like(gr)

    key = lax.broadcasted_iota(jnp.int32, (1, K_ALL), 1)
    in_mid = key < K_MID
    in_left = key < K_MID + K_BAND
    slot = key & (SLOTS - 1)
    key_row = jnp.where(
        in_mid,
        key // TW,
        jnp.where(in_left, (key - K_MID) // SLOTS, (key - K_MID - K_BAND) // SLOTS),
    )
    band_col = jnp.where(in_left, slot, TW + DEPTH + slot)
    key_col = jnp.where(in_mid, (key & (TW - 1)) + DEPTH, jnp.where(slot < DEPTH, band_col, 1000))
    col_image = tile_col * TW + key_col - DEPTH
    key_col = jnp.where((col_image >= 0) & (col_image < IMG_W), key_col, 1000)
    token = lax.broadcasted_iota(jnp.int32, (BLK, 1), 0)
    row_off = key_row - token // TW
    col_off = key_col - (token & (TW - 1))
    near = (row_off >= 0) & (row_off < 7) & (col_off >= 0) & (col_off < 7)
    row_image = tile_row * TH + key_row - DEPTH

    def start(b):
        rows, m_rows, b_rows = block_of(b)
        kk = jnp.concatenate([mid[0, m_rows], from_left[0, b_rows], from_right[0, b_rows]], axis=0)
        vv = jnp.concatenate([mid[1, m_rows], from_left[1, b_rows], from_right[1, b_rows]], axis=0)
        qs = stacked(q[rows, :] * jnp.asarray(HD**-0.5, BF16))
        gs = stacked(ga[rows, :])
        return kk, vv, qs, gs, dot(qs, kk, 1, 1), dot(gs, vv, 1, 1)

    def soften(b, kk, vv, qs, gs, s, dprob):
        row_here = row_image + b * BLK_ROWS
        valid = near & (row_here >= 0) & (row_here < IMG_H)
        bias = jnp.where(valid, 0.0, -jnp.inf).astype(F32)
        s = (s.reshape(HEADS_HERE, BLK, K_ALL) + bias[None]).reshape(HEADS_HERE * BLK, K_ALL)
        e = jnp.exp(s - jnp.max(s, axis=1, keepdims=True))
        p = e * (1.0 / jnp.sum(e, axis=1, keepdims=True))
        return kk, vv, qs, gs, dprob, p, p.astype(BF16)

    def apply(b, kk, vv, qs, gs, dprob, p, p16):
        return kk, qs, gs, dprob, p, dot(p16, vv, 1, 0).astype(BF16), dot(p16, gs, 0, 0)

    def finish(b, kk, qs, gs, dprob, p, attn, grad_v):
        rows, m_rows, b_rows = block_of(b)
        attn_out[rows, :] = unstacked(attn)
        delta = jnp.sum(gs.astype(F32) * attn.astype(F32), axis=1, keepdims=True)
        return kk, qs, (p * (dprob - delta)).astype(BF16), grad_v

    def spill(b, kk, qs, ds, grad_v):
        rows, m_rows, b_rows = block_of(b)
        grad_q[rows, :] = unstacked(dot(ds, kk, 1, 0) * (HD**-0.5)).astype(BF16)
        for i, g in enumerate((dot(ds, qs, 0, 0), grad_v)):
            grad_mid[i, m_rows] += g[:K_MID]
            gl[i, b_rows] += g[K_MID : K_MID + K_BAND]
            gr[i, b_rows] += g[K_MID + K_BAND :]

    stages = (start, soften, apply, finish, spill)
    held = {b: () for b in range(BLOCKS)}
    for step in range(BLOCKS + len(stages) - 1):
        for i, stage in enumerate(stages):
            if 0 <= step - i < BLOCKS:
                held[step - i] = stage(step - i, *held[step - i])

    joining = spread(1)
    for i in range(2):
        band_left[i] = dot(joining, gl[i].astype(BF16), 1, 0).astype(BF16)
        band_right[i] = dot(joining, gr[i].astype(BF16), 1, 0).astype(BF16)


def slot(yx):
    return (yx // X) * X + (yx % 2) * 2 + (yx % X) // 2


def put_term(out, term):
    term = term.astype(BF16)
    for yx in range(YH * X):
        for z in range(Z):
            at = (z * YH * X + yx) * 16
            out[slot(yx), z] = term[at : at + 16]


def hidden_kernel(after, h0, h1, h2, h3, hidden, to_above, to_below):
    head = head_index()
    for i, piece in enumerate((h0, h1, h2, h3)):
        hidden[pl.ds(pl.multiple_of((head ^ i) * PIECE, PIECE), PIECE), :] = piece[...]
    to_above[...] = hidden[:EDGE, :]
    to_below[...] = hidden[TOKENS - EDGE :, :]


def first_terms_kernel(grad_q, attn, g0, g1, g2, g3, hidden, out, og, terms, sems):
    head = head_index()
    for i, piece in enumerate((g0, g1, g2, g3)):
        og[pl.ds(pl.multiple_of((head ^ i) * PIECE, PIECE), PIECE), :] = piece[...]
    copies = []
    for i, (left, right) in enumerate(((hidden, grad_q), (og, attn))):
        put_term(terms.at[i], dot(left[...], right[...], 0, 0))
        copies.append(pltpu.make_async_copy(terms.at[i], out.at[:, i], sems.at[i]))
        copies[-1].start()
    for copy in copies:
        copy.wait()


def second_terms_kernel(
    grad_mid, from_left, from_right, hidden, hid_above, hid_below, first,
    out, grads, top, bottom, to_above, to_below,
    hid_mid, terms, sems,
):
    hid_mid[:EDGE] = hid_above[...]
    hid_mid[EDGE : EDGE + TOKENS] = hidden[...]
    hid_mid[EDGE + TOKENS :] = hid_below[...]
    left = pick(0, 0)
    right = pick(TW - DEPTH, 0)
    both = []
    for i in range(2):
        g = grad_mid[i] + dot(left, from_left[i], 1, 0) + dot(right, from_right[i], 1, 0)
        both.append(g.astype(BF16))
        to_above[i] = both[i][:EDGE]
        grads[i] = both[i][EDGE : EDGE + TOKENS]
        top[i] = g[EDGE : 2 * EDGE]
        bottom[i] = g[TOKENS : TOKENS + EDGE]
        to_below[i] = both[i][EDGE + TOKENS :]
    both = jnp.concatenate(both, axis=1)
    copies = []
    width = D // CHUNKS
    deep = Z // CHUNKS
    for c in range(CHUNKS):
        term = dot(hid_mid[:, c * width : (c + 1) * width], both, 0, 0).astype(BF16)
        for i in range(2):
            for yx in range(YH * X):
                for z in range(deep):
                    at = (z * YH * X + yx) * 16
                    here = term[at : at + 16, i * FEAT : (i + 1) * FEAT]
                    terms[i, slot(yx), c * deep + z] = here
        part = pl.ds(c * deep, deep)
        for i in range(2):
            copies.append(
                pltpu.make_async_copy(
                    terms.at[i, :, part], out.at[:, 2 + i, part], sems.at[2 * c + i]
                )
            )
            copies[-1].start()
    for copy in copies:
        copy.wait()


def hidden_grad_kernel(
    grad_q, inner, top, bottom, from_above, from_below, w_qkv_in, keep, send, grads, w_qkv, sem
):
    copy = pltpu.make_async_copy(w_qkv_in, w_qkv, sem)
    copy.start()
    core = lax.axis_index("core")
    for i in range(2):
        grads[i, :EDGE] = (top[i] + from_above[i].astype(F32)).astype(BF16)
        grads[i, EDGE : TOKENS - EDGE] = inner[i, EDGE : TOKENS - EDGE]
        grads[i, TOKENS - EDGE :] = (bottom[i] + from_below[i].astype(F32)).astype(BF16)
    copy.wait()
    for yl in range(YL):
        for out, c in ((send, 1 - core), (keep, core)):
            at = pl.ds(pl.multiple_of((yl * CORE + c) * PIECE, PIECE), PIECE)
            total = dot(grad_q[at, :], w_qkv[0], 1, 1)
            for j in range(2):
                total += dot(grads[j, at, :], w_qkv[1 + j], 1, 1)
            out[yl] = total.astype(BF16)


def halve_kernel(keep, got, stay, send):
    yl = lax.axis_index("yl")
    stay[...] = keep[yl].astype(F32) + got[yl].astype(F32)
    send[...] = (keep[1 - yl].astype(F32) + got[1 - yl].astype(F32)).astype(BF16)


def summed(terms):
    total = terms[0].astype(F32)
    for i in range(1, 8):
        total += terms[i].astype(F32)
    return total


def sum_kernel(terms, out):
    for j in range(4):
        total = terms[0, j].astype(F32)
        for i in range(1, YH * X):
            total += terms[i, j].astype(F32)
        for z in range(Z):
            at = (z % 2) * (Z // 2) + z // 2
            out[at, :, j * FEAT : (j + 1) * FEAT] = total[z].astype(BF16)


def last_kernel(parts, grad_wqkv, grad_wout):
    total = summed(parts)
    grad_wqkv[0] = total[:, :FEAT]
    grad_wout[...] = total[:, FEAT : 2 * FEAT]
    grad_wqkv[1] = total[:, 2 * FEAT : 3 * FEAT]
    grad_wqkv[2] = total[:, 3 * FEAT :]


def ring(size, step):
    return [(i, (i + step) % size) for i in range(size)]


SWAP = [(0, 1), (1, 0)]
COLS = ("yh", "xh", "xl", "yl")


def columns(step):
    pairs = []
    for col in range(YH * X):
        for yl in range(YL):
            to = col + step
            to_yl = yl if 0 <= to < YH * X else 1 - yl
            pairs.append((col * YL + yl, (to % (YH * X)) * YL + to_yl))
    return pairs


def per_device(hidden_in, queries, keys, values, w_qkv, w_out, out_grad):
    q = queries.reshape(TOKENS, FEAT)
    k = keys.reshape(TOKENS, FEAT)
    v = values.reshape(TOKENS, FEAT)
    w3 = w_qkv.transpose(1, 0, 2)

    flat = shaped((TOKENS, FEAT))
    edge = shaped((2, EDGE, FEAT))
    band = shaped((2, SENT, FEAT))
    mids = shaped((2, CENTER, FEAT))
    own = shaped((PIECE, D))
    own_grad = out_grad.reshape(PIECE, D)
    own_hidden = hidden_in.reshape(PIECE, D)
    to_above, to_below = call(
        edges_kernel, (edge, edge), scratch=[pltpu.SemaphoreType.DMA((4,))], n_in=2, hbm=(0, 1)
    )(k, v)
    below = lax.ppermute(to_above, ZZ, ring(Z, -1))
    above = lax.ppermute(to_below, ZZ, ring(Z, 1))
    q, kv, w_out, g0, h0 = call(
        load_kernel,
        (flat, shaped((2, TOKENS, FEAT)), shaped((FEAT, D)), own, own),
        scratch=[pltpu.SemaphoreType.DMA((6,))],
        n_in=7,
        hbm=range(1, 7),
        flops=10_000_000_000,
    )(to_above, q, k, v, w_out, own_grad, own_hidden)
    g2 = lax.ppermute(own_grad, "yl", SWAP)
    late, _ = lax.optimization_barrier((own_hidden, below))
    h2 = lax.ppermute(late, "yl", SWAP)

    mid, to_left, to_right = call(bands_kernel, (mids, band, band), n_in=3)(kv, above, below)
    from_right = lax.ppermute(to_left, COLS, columns(-1))
    from_left = lax.ppermute(to_right, COLS, columns(1))
    g2, _ = lax.optimization_barrier((g2, to_left))
    g3 = lax.ppermute(g2, "core", SWAP)
    g1 = lax.ppermute(g0, "core", SWAP)
    h1 = lax.ppermute(h0, "core", SWAP)
    h2, _, _ = lax.optimization_barrier((h2, from_left, from_right))
    h3 = lax.ppermute(h2, "core", SWAP)

    attn, grad_q, grad_mid, band_left, band_right = call(
        attention_kernel,
        (flat, flat, shaped((2, CENTER, FEAT), F32), band, band),
        scratch=[
            pltpu.VMEM((TOKENS, FEAT), BF16),
            pltpu.VMEM((2, BAND, FEAT), F32),
            pltpu.VMEM((2, BAND, FEAT), F32),
            pltpu.VMEM((2, BAND, FEAT), BF16),
            pltpu.VMEM((2, BAND, FEAT), BF16),
        ],
        n_in=9,
    )(q, g0, g1, g2, g3, w_out, mid, from_left, from_right)

    got_right = lax.ppermute(band_left, COLS, columns(-1))
    got_left = lax.ppermute(band_right, COLS, columns(1))
    hid_edge = shaped((EDGE, D))
    hidden, to_above, to_below = call(
        hidden_kernel, (shaped((TOKENS, D)), hid_edge, hid_edge), n_in=5
    )(band_left, h0, h1, h2, h3)
    hid_below = lax.ppermute(to_above, ZZ, ring(Z, -1))
    hid_above = lax.ppermute(to_below, ZZ, ring(Z, 1))
    all_terms = shaped((YH * X, 4, Z, 16, FEAT))
    (terms,) = call(
        first_terms_kernel,
        (all_terms,),
        scratch=[
            pltpu.VMEM((TOKENS, D), BF16),
            pltpu.VMEM((2, YH * X, Z, 16, FEAT), BF16),
            pltpu.SemaphoreType.DMA((2,)),
        ],
        n_in=7,
        hbm_out=(0,),
        flops=10_000_000_000,
    )(grad_q, attn, g0, g1, g2, g3, hidden)
    edge32 = shaped((2, EDGE, FEAT), F32)
    terms, grads, top, bottom, to_above, to_below = call(
        second_terms_kernel,
        (all_terms, shaped((2, TOKENS, FEAT)), edge32, edge32, edge, edge),
        scratch=[
            pltpu.VMEM((CENTER, D), BF16),
            pltpu.VMEM((2, YH * X, Z, 16, FEAT), BF16),
            pltpu.SemaphoreType.DMA((2 * CHUNKS,)),
        ],
        n_in=7,
        hbm=(6,),
        hbm_out=(0,),
        alias={6: 0},
    )(grad_mid, got_left, got_right, hidden, hid_above, hid_below, terms)
    got_below = lax.ppermute(to_above, ZZ, ring(Z, -1))
    got_above = lax.ppermute(to_below, ZZ, ring(Z, 1))
    terms = lax.all_to_all(terms, ("yh", "xl", "xh"), 0, 0, tiled=True)

    half = shaped((YL, PIECE, D))
    keep, send = call(
        hidden_grad_kernel,
        (half, half),
        scratch=[
            pltpu.VMEM((2, TOKENS, FEAT), BF16),
            pltpu.VMEM((3, D, FEAT), BF16),
            pltpu.SemaphoreType.DMA,
        ],
        n_in=7,
        hbm=(6,),
    )(grad_q, grads, top, bottom, got_above, got_below, w3)
    got = lax.ppermute(send, "core", SWAP)
    stay, send = call(halve_kernel, (shaped((PIECE, D), F32), shaped((PIECE, D))), n_in=2)(keep, got)
    got = lax.ppermute(send, "yl", SWAP)
    grad_hidden = (stay + got.astype(F32)).astype(BF16).reshape(1, 8, TW, D)

    (parts,) = call(sum_kernel, (shaped((Z, 16, 4 * FEAT)),), n_in=1)(terms)
    parts = lax.all_to_all(parts, ("zl", "zh"), 0, 0, tiled=True)
    grad_wqkv, grad_wout = call(
        last_kernel, (shaped((3, 16, FEAT), F32), shaped((16, FEAT), F32)), n_in=1
    )(parts)
    return grad_hidden, grad_wqkv.transpose(1, 0, 2), grad_wout.T


def solution(mesh):
    fine = Mesh(mesh.devices.reshape(Z // 2, 2, YH, 2, 2, YL, CORE), GRID + HEAD)
    return jax.shard_map(
        per_device,
        mesh=fine,
        in_specs=(
            P(GRID, HEAD, None, None),
            P(GRID, None, None, HEAD),
            P(GRID, None, None, HEAD),
            P(GRID, None, None, HEAD),
            P(None, None, HEAD),
            P(HEAD, None),
            P(GRID, HEAD, None, None),
        ),
        out_specs=(P(GRID, HEAD, None, None), P(GRID, None, HEAD), P(HEAD, GRID)),
        check_vma=False,
    )
```
